32 devices in a mesh: ctx: 16 (over z, x, core), head: 2 (over y).
Axes of the slice: x: 2, y: 2, z: 4, core: 2. Of those that a mesh axis runs over, the one named last changes fastest.
Arguments:
- queries: bfloat16 [4096, 2048], P('ctx', 'head'), may hold values from -40 to 40
- keys: bfloat16 [4096, 2048], P('ctx', 'head'), may hold values from -4 to 4
- values: bfloat16 [4096, 2048], P('ctx', 'head'), may hold values from -5 to 5
- selected: int32 [16, 128, 3], P('head', 'ctx'), may hold values from 0 to 15, as said below
- out_weight: bfloat16 [2048, 2048], P(None, 'head'), may hold values from -0.125 to 0.125
Outputs:
- projected: bfloat16 [4096, 2048], P('ctx', 'head')
The draws below stay inside these ranges and needn't reach their ends.
Inputs may be any that keep to these rules, and one draw needn't show every extreme that they name: `selected`: entry 0 of a tile's selection is its own block; entries 1 and 2 are two different earlier blocks, or both the own block where no earlier block is chosen for the tile (one earlier block and the own block in the second key block). For each head, the tiles of one key block name any one other block at most 2 times, and exactly 2 times for every block they name, from the third key block on.
All inputs are finite; a program needn't handle non-finite values.
Results may differ from the reference program's by a relative error of at most 0.0054.
Values may be sent and summed in bfloat16 or wider, within the bound.
A program may use at most 64 MiB of HBM per device.

```python
import jax
import jax.numpy as jnp
from jax import lax

HEADS = 16
HEAD_DIM = 128
D = 2048
TILE = 32
TOPK = 3
BLOCK = 256
CONTEXT = 4096


def paired_fields(key):
    shape = (CONTEXT, HEADS * HEAD_DIM)
    keys = jnp.clip(jax.random.normal(jax.random.fold_in(key, 11), shape, jnp.float32), -4.0, 4.0)
    queries = jnp.clip(jax.random.normal(jax.random.fold_in(key, 12), shape, jnp.float32), -4.0, 4.0)
    return (keys, queries)


def draw_keys(key, part):
    return paired_fields(key)[0].astype(jnp.bfloat16)


def draw_queries(key, part):
    return paired_fields(key)[1].astype(jnp.bfloat16)


def draw_selected(key, part):
    tile_quantity = CONTEXT // BLOCK
    nt = BLOCK // TILE
    unscaled_logits = jax.random.randint(jax.random.fold_in(key, 21), (HEADS, tile_quantity, tile_quantity), 0, 4096)
    anchor_tile = jax.random.randint(jax.random.fold_in(key, 22), (HEADS, tile_quantity, 1), 0, 8192)
    key_position_number = jnp.arange(tile_quantity, dtype=jnp.int32)
    holder_rank = key_position_number[:, None]
    logit_increment = jnp.where(key_position_number[None, None, :] == 0, anchor_tile, 0) + jnp.where(key_position_number[None, :] == holder_rank - 1, 3000, 0)[None]
    preceding_filter = (key_position_number[None, :] < holder_rank)[None]
    group_relevance = jnp.where(preceding_filter, (unscaled_logits + logit_increment) * tile_quantity + key_position_number, -1 - key_position_number)
    order = jnp.argsort(-group_relevance, axis=-1).astype(jnp.int32)
    count = jnp.minimum(key_position_number, nt)
    safe = jnp.maximum(count, 1)
    slots = jnp.arange(nt, dtype=jnp.int32)
    first_pos = jnp.broadcast_to((slots[None, :] % safe[:, None])[None], (HEADS, tile_quantity, nt))
    second_pos = jnp.broadcast_to(((slots[None, :] + 1) % safe[:, None])[None], (HEADS, tile_quantity, nt))
    first = jnp.take_along_axis(order, first_pos, axis=-1)
    second = jnp.take_along_axis(order, second_pos, axis=-1)
    own = jnp.broadcast_to(holder_rank[None], (HEADS, tile_quantity, nt))
    live = (slots[None, :] < count[:, None])[None]
    pick_one = jnp.where(live, first, own)
    pick_two = jnp.where(jnp.logical_and(live, (count[:, None] >= 2)[None]), second, own)
    ranks_raw = jax.random.randint(jax.random.fold_in(key, 23), (HEADS, tile_quantity, nt), 0, 2 ** 20) * nt + slots
    ranks = jnp.argsort(jnp.argsort(ranks_raw, axis=-1), axis=-1).astype(jnp.int32)
    pick_one = jnp.take_along_axis(pick_one, ranks, axis=-1)
    pick_two = jnp.take_along_axis(pick_two, ranks, axis=-1)
    chosen = jnp.stack([own, pick_one, pick_two], axis=-1)
    return chosen.reshape(HEADS, tile_quantity * nt, TOPK).astype(jnp.int32)


def shard_levels(stream_key, shape, pieces, smallest, largest):
    gain = 1.0
    for axis_at, blocks in pieces:
        draws = jax.random.uniform(jax.random.fold_in(jax.random.fold_in(stream_key, 6), axis_at), (blocks,), jnp.float32, smallest / len(pieces), largest / len(pieces))
        gain = gain * jnp.repeat(jnp.exp(draws), shape[axis_at] // blocks).reshape((-1,) + (1,) * (len(shape) - 1 - axis_at))
    return gain


def centred(stream_key, extent, spread, reach, cuts=(), kind=jnp.bfloat16):
    result = jax.random.normal(stream_key, extent, jnp.float32) * spread
    if len(cuts) > 0:
        result = shard_levels(stream_key, extent, cuts, -0.22, 0.18) * result
    return jnp.clip(result, min=-reach, max=reach).astype(kind)


def setup_inputs(seed: int = 0) -> dict:
    arg_keys = jax.random.split(jax.random.key(seed), 6)
    return {
        "queries": draw_queries(jax.random.fold_in(arg_keys[5], 71), 0),
        "keys": draw_keys(jax.random.fold_in(arg_keys[5], 71), 0),
        "values": centred(arg_keys[2], (CONTEXT, HEADS * HEAD_DIM), 1.0, 5.0, ((0, 16), (1, 2))),
        "selected": draw_selected(jax.random.fold_in(arg_keys[5], 71), 0),
        "out_weight": centred(arg_keys[4], (HEADS * HEAD_DIM, D), (HEADS * HEAD_DIM) ** -0.5, 0.125, ((1, 2),)),
    }


def reference(queries, keys, values, selected, out_weight):
    tile_quantity = CONTEXT // BLOCK
    nt = BLOCK // TILE
    scale = HEAD_DIM ** -0.5
    qb = queries.reshape(tile_quantity, nt, TILE, HEADS, HEAD_DIM)
    kb = keys.reshape(tile_quantity, BLOCK, HEADS, HEAD_DIM)
    vb = values.reshape(tile_quantity, BLOCK, HEADS, HEAD_DIM)
    sb = jnp.transpose(selected.reshape(HEADS, tile_quantity, nt, TOPK), (1, 0, 2, 3))
    pos = jnp.arange(BLOCK, dtype=jnp.int32)
    causal = (pos[:, None] >= pos[None, :]).reshape(nt, TILE, BLOCK)
    head_ids = jnp.arange(HEADS, dtype=jnp.int32)

    def finish(scores, vals_f, form):
        top = jnp.max(scores, axis=-1)
        prob = jnp.exp(scores - top[..., None])
        total = jnp.sum(prob, axis=-1)
        weights = prob.astype(jnp.bfloat16).astype(jnp.float32)
        part = jnp.einsum(form, weights, vals_f) / total[..., None]
        return part, top + jnp.log(total)

    def one_block(b):
        query = qb[b].astype(jnp.float32)
        own_k = kb[b].astype(jnp.float32)
        own_v = vb[b].astype(jnp.float32)
        s0 = jnp.einsum('ntha,kha->hntk', query, own_k) * scale
        s0 = jnp.where(causal[None], s0, jnp.float32(-1e30))
        out0, lse0 = finish(s0, own_v, 'hntk,kha->hnta')
        top = lse0
        kept = []
        for r in range(1, TOPK):
            picks = sb[b, :, :, r]
            sel_k = kb[picks, :, head_ids[:, None], :].astype(jnp.float32)
            sel_v = vb[picks, :, head_ids[:, None], :].astype(jnp.float32)
            s = jnp.einsum('ntha,hnka->hntk', query, sel_k) * scale
            part, lse = finish(s, sel_v, 'hntk,hnka->hnta')
            valid = (picks != b)[:, :, None]
            kept.append((part, lse, valid))
            top = jnp.maximum(top, jnp.where(valid, lse, lse0))
        w0 = jnp.exp(lse0 - top)
        num = w0[..., None] * out0
        den = w0
        for part, lse, valid in kept:
            w = jnp.exp(jnp.where(valid, lse - top, jnp.float32(-1e30)))
            num = num + w[..., None] * part
            den = den + w
        att = num / den[..., None]
        att = jnp.transpose(att, (1, 2, 0, 3)).reshape(BLOCK, HEADS * HEAD_DIM)
        return att.astype(jnp.bfloat16)

    attention = lax.map(one_block, jnp.arange(tile_quantity, dtype=jnp.int32))

    def project(rows):
        return jnp.dot(rows, out_weight, preferred_element_type=jnp.float32).astype(jnp.bfloat16)

    projected = lax.map(project, attention)
    return projected.reshape(CONTEXT, D)
```

```python
import functools

import jax
import jax.numpy as jnp
from jax import lax
from jax.experimental import pallas as pl
from jax.experimental.pallas import tpu as pltpu
from jax.sharding import PartitionSpec as P

CAP = 2
MESH = pl.DeviceIdType.MESH
NT = (((1,), (1,)), ((), ()))


def softmax_block(query, key, value, scale, mask):
    scores = lax.dot_general(query, key, NT, preferred_element_type=jnp.float32) * scale
    if mask is not None:
        scores = jnp.where(mask, scores, jnp.float32(-1e30))
    top = jnp.max(scores, axis=-1, keepdims=True)
    prob = jnp.exp(scores - top)
    total = jnp.sum(prob, axis=-1, keepdims=True)
    part = jnp.dot(prob.astype(jnp.bfloat16), value, preferred_element_type=jnp.float32)
    return part * (1.0 / total), top + jnp.log(total)


def kernel(
    dims,
    tbl,
    q_hbm,
    k_hbm,
    v_hbm,
    w_hbm,
    out_ref,
    q,
    k,
    v,
    w,
    qsend,
    osend,
    ssend,
    own,
    own_lse,
    att,
    acc,
    load_sem,
    qs_sem,
    qr_sem,
    os_sem,
    or_sem,
    ss_sem,
    sr_sem,
    as_sem,
    ar_sem,
    *grouped,
):
    n, nh, heads, tiles, rows, width, groups = dims
    per = heads // groups
    tokens = tiles * rows
    scale = width ** (-0.5)
    qrecv, orecv, srecv, lse_cols = (
        grouped[i * groups : (i + 1) * groups] for i in range(4)
    )
    me = lax.axis_index("ctx")
    hd = lax.axis_index("head")
    pick_at = n * heads * CAP
    slot_at = pick_at + heads * tiles * 2

    loads = [
        pltpu.make_async_copy(src, dst, load_sem.at[i])
        for i, (src, dst) in enumerate(((q_hbm, q), (k_hbm, k), (v_hbm, v), (w_hbm, w)))
    ]
    for copy in loads:
        copy.start()

    barrier = pltpu.get_barrier_semaphore()

    def greet(d, _):
        pl.semaphore_signal(
            barrier, inc=1, device_id={"ctx": lax.rem(me + d, n)}, device_id_type=MESH
        )
        return 0

    lax.fori_loop(1, n, greet, 0)
    for j in range(1, nh):
        pl.semaphore_signal(
            barrier, inc=1, device_id={"head": lax.rem(hd + j, nh)}, device_id_type=MESH
        )

    def distance(i):
        half = (i + 1) // 2
        return n // 2 + jnp.where(i % 2 == 0, half, -half)

    def q_copy(g, there, here):
        return pltpu.make_async_remote_copy(
            src_ref=qsend.at[g, there],
            dst_ref=qrecv[g].at[here],
            send_sem=qs_sem.at[g, there],
            recv_sem=qr_sem.at[g, here],
            device_id={"ctx": there},
            device_id_type=MESH,
        )

    def o_copy(g, there, here):
        return pltpu.make_async_remote_copy(
            src_ref=osend.at[g, there],
            dst_ref=orecv[g].at[here],
            send_sem=os_sem.at[g, there],
            recv_sem=or_sem.at[g, here],
            device_id={"ctx": there},
            device_id_type=MESH,
        )

    def s_copy(g, there, here):
        return pltpu.make_async_remote_copy(
            src_ref=ssend.at[g, there],
            dst_ref=srecv[g].at[here],
            send_sem=ss_sem.at[g, there],
            recv_sem=sr_sem.at[g, here],
            device_id={"ctx": there},
            device_id_type=MESH,
        )

    def a_copy(g, there, here):
        return pltpu.make_async_remote_copy(
            src_ref=att.at[here, g],
            dst_ref=att.at[here, g],
            send_sem=as_sem.at[there, g],
            recv_sem=ar_sem.at[here, g],
            device_id={"head": there},
            device_id_type=MESH,
        )

    loads[0].wait()
    pl.semaphore_wait(barrier, n - 1 + nh - 1)

    for g in range(groups):

        def send_queries(i, _, g=g):
            there = me - distance(i)

            @pl.when(there >= 0)
            def _():
                for hh in range(per):
                    h = g * per + hh
                    for s in range(CAP):
                        tile = tbl[(there * heads + h) * CAP + s]
                        qsend[g, there, hh, s] = q[tile, :, h * width : (h + 1) * width]
                q_copy(g, there, me).start()

            return 0

        lax.fori_loop(0, n - 1, send_queries, 0)

    loads[1].wait()
    loads[2].wait()
    lane = lax.broadcasted_iota(jnp.int32, (tokens, 128), 1)
    causal = lax.broadcasted_iota(jnp.int32, (tokens, tokens), 0) >= lax.broadcasted_iota(
        jnp.int32, (tokens, tokens), 1
    )
    lses = jnp.zeros((tokens, 128), jnp.float32)
    for h in range(heads):
        cols = slice(h * width, (h + 1) * width)
        query = q[:, :, cols].reshape(tokens, width)
        part, lse = softmax_block(query, k[:, cols], v[:, cols], scale, causal)
        own[h] = part.reshape(tiles, rows, width)
        lses = jnp.where(lane == h, lse, lses)
    own_lse[...] = lses.reshape(tiles, rows, 128)

    short = CAP * rows
    lane_short = lax.broadcasted_iota(jnp.int32, (short, 128), 1)
    for g in range(groups):
        orecv[g][me] = jnp.zeros((per, CAP, rows, width), jnp.bfloat16)

        def answer(i, _, g=g):
            there = me + distance(i)

            @pl.when(there < n)
            def _():
                q_copy(g, me, there).wait_recv()
                stats = jnp.zeros((short, 128), jnp.float32)
                for hh in range(per):
                    h = g * per + hh
                    cols = slice(h * width, (h + 1) * width)
                    query = qrecv[g][there, hh].reshape(short, width)
                    part, lse = softmax_block(query, k[:, cols], v[:, cols], scale, None)
                    osend[g, there, hh] = part.astype(jnp.bfloat16).reshape(CAP, rows, width)
                    stats = jnp.where(lane_short == hh, lse, stats)
                stats = jnp.concatenate([stats, jnp.zeros((128 - short, 128), jnp.float32)], 0)
                ssend[g, there] = jnp.transpose(stats)[:8]
                o_copy(g, there, me).start()
                s_copy(g, there, me).start()

            return 0

        lax.fori_loop(0, n - 1, answer, 0)

    loads[3].wait()
    part_cols = min(256, out_ref.shape[1])

    def project(p, g, first):
        def body(c, _):
            at = pl.ds(pl.multiple_of(c * part_cols, part_cols), part_cols)
            term = jnp.dot(att[p, g], w[p, g, :, at], preferred_element_type=jnp.float32)
            if first:
                acc[:, at] = term
            else:
                acc[:, at] += term
            return 0

        lax.fori_loop(0, out_ref.shape[1] // part_cols, body, 0)

    for g in range(groups):
        lse_cols[g][me] = jnp.full((CAP, rows, 8), -1e30, jnp.float32)

        def collect(i, _, g=g):
            there = me - distance(i)

            @pl.when(there >= 0)
            def _():
                s_copy(g, me, there).wait_recv()
                lse_cols[g][there] = jnp.transpose(srecv[g][there])[:short].reshape(CAP, rows, 8)
                o_copy(g, me, there).wait_recv()

            return 0

        lax.fori_loop(0, n - 1, collect, 0)

        def combine(t, _, g=g):
            for hh in range(per):
                h = g * per + hh
                at = (h * tiles + t) * 2
                a1, a2 = tbl[pick_at + at], tbl[pick_at + at + 1]
                s1, s2 = tbl[slot_at + at], tbl[slot_at + at + 1]
                l0 = own_lse[t, :, h : h + 1]
                l1 = lse_cols[g][a1, s1][:, hh : hh + 1]
                l2 = lse_cols[g][a2, s2][:, hh : hh + 1]
                top = jnp.maximum(l0, jnp.maximum(l1, l2))
                w0, w1, w2 = jnp.exp(l0 - top), jnp.exp(l1 - top), jnp.exp(l2 - top)
                inv = 1.0 / (w0 + w1 + w2)
                o1 = orecv[g][a1, hh, s1].astype(jnp.float32)
                o2 = orecv[g][a2, hh, s2].astype(jnp.float32)
                mixed = (w0 * inv) * own[h, t] + (w1 * inv) * o1 + (w2 * inv) * o2
                att[hd, g, pl.ds(pl.multiple_of(t * rows, rows), rows), hh * width : (hh + 1) * width] = (
                    mixed.astype(jnp.bfloat16)
                )
            return 0

        lax.fori_loop(0, tiles, combine, 0)
        for j in range(1, nh):
            a_copy(g, lax.rem(hd + j, nh), hd).start()

    for g in range(groups):
        project(hd, g, g == 0)
    for g in range(groups):
        for j in range(1, nh):
            peer = lax.rem(hd + j, nh)
            a_copy(g, hd, peer).wait_recv()
            project(peer, g, False)
    out_ref[...] = acc[...].astype(out_ref.dtype)

    for g in range(groups):

        def drain(i, _, g=g):
            d = distance(i)

            @pl.when(me - d >= 0)
            def _():
                q_copy(g, me - d, me).wait_send()

            @pl.when(me + d < n)
            def _():
                o_copy(g, me + d, me).wait_send()
                s_copy(g, me + d, me).wait_send()

            return 0

        lax.fori_loop(0, n - 1, drain, 0)
        for j in range(1, nh):
            a_copy(g, lax.rem(hd + j, nh), hd).wait_send()


def tables(selected, n):
    heads, tiles, _ = selected.shape
    picks = selected[:, :, 1:].reshape(heads, tiles * 2)
    order = jnp.arange(tiles * 2, dtype=jnp.int32)
    same = (picks[:, :, None] == picks[:, None, :]) & (order[None, :] < order[:, None])
    slot = jnp.minimum(jnp.sum(same.astype(jnp.int32), axis=-1), CAP - 1)
    hit = (picks[None, :, None, :] == jnp.arange(n, dtype=jnp.int32)[:, None, None, None]) & (
        slot[None, :, None, :] == jnp.arange(CAP, dtype=jnp.int32)[None, None, :, None]
    )
    tile = jnp.max(jnp.where(hit, order // 2, 0), axis=-1)
    return jnp.concatenate([tile.reshape(-1), picks.reshape(-1), slot.reshape(-1)])


def solution(mesh):
    n, nh = mesh.shape["ctx"], mesh.shape["head"]

    def local(queries, keys, values, selected, out_weight):
        heads, tiles = selected.shape[:2]
        tokens, cols = queries.shape[0], out_weight.shape[1]
        width = queries.shape[1] // heads
        rows = tokens // tiles
        groups = 2 if heads % 2 == 0 and heads >= 4 else 1
        per = heads // groups
        bf16, f32 = jnp.bfloat16, jnp.float32
        dma = pltpu.SemaphoreType.DMA
        packet = (n, per, CAP, rows, width)
        grouped = (
            [pltpu.VMEM(packet, bf16)] * (2 * groups)
            + [pltpu.VMEM((n, 8, 128), f32)] * groups
            + [pltpu.VMEM((n, CAP, rows, 8), f32)] * groups
        )
        weight = out_weight.reshape(nh, groups, per * width, cols)
        return pl.pallas_call(
            functools.partial(kernel, (n, nh, heads, tiles, rows, width, groups)),
            out_shape=jax.ShapeDtypeStruct((tokens, cols), bf16),
            in_specs=[pl.BlockSpec(memory_space=pltpu.SMEM)]
            + [pl.BlockSpec(memory_space=pl.ANY)] * 4,
            out_specs=pl.BlockSpec(memory_space=pltpu.VMEM),
            scratch_shapes=[
                pltpu.VMEM((tiles, rows, heads * width), bf16),
                pltpu.VMEM((tokens, heads * width), bf16),
                pltpu.VMEM((tokens, heads * width), bf16),
                pltpu.VMEM(weight.shape, bf16),
                pltpu.VMEM((groups,) + packet, bf16),
                pltpu.VMEM((groups,) + packet, bf16),
                pltpu.VMEM((groups, n, 8, 128), f32),
                pltpu.VMEM((heads, tiles, rows, width), f32),
                pltpu.VMEM((tiles, rows, 128), f32),
                pltpu.VMEM((nh, groups, tokens, per * width), bf16),
                pltpu.VMEM((tokens, cols), f32),
                dma((4,)),
                dma((groups, n)),
                dma((groups, n)),
                dma((groups, n)),
                dma((groups, n)),
                dma((groups, n)),
                dma((groups, n)),
                dma((nh, groups)),
                dma((nh, groups)),
            ]
            + grouped,
            compiler_params=pltpu.CompilerParams(
                collective_id=0, has_side_effects=True, vmem_limit_bytes=56 * 1024 * 1024
            ),
        )(
            tables(selected, n),
            queries.reshape(tiles, rows, heads * width),
            keys,
            values,
            weight,
        )

    return jax.shard_map(
        local,
        mesh=mesh,
        in_specs=(
            P("ctx", "head"),
            P("ctx", "head"),
            P("ctx", "head"),
            P("head", "ctx", None),
            P(None, "head"),
        ),
        out_specs=P("ctx", "head"),
        check_vma=False,
    )
```

```python
import functools

import jax
import jax.numpy as jnp
from jax import lax
from jax.experimental import pallas as pl
from jax.experimental.pallas import tpu as pltpu
from jax.sharding import PartitionSpec as P

CAP = 2
AHEAD = 2
LAG = 2
MESH = pl.DeviceIdType.MESH
LOG2E = 1.4426950408889634
NT = (((1,), (1,)), ((), ()))


def softmax_block(query, key, value, scale, mask):
    scores = lax.dot_general(query, key, NT, preferred_element_type=jnp.float32)
    if mask is not None:
        scores = jnp.where(mask, scores, jnp.float32(-1e30))
    top = jnp.max(scores, axis=-1, keepdims=True)
    prob = jnp.exp2((scores - top) * (scale * LOG2E))
    total = jnp.sum(prob, axis=-1, keepdims=True)
    part = jnp.dot(prob.astype(jnp.bfloat16), value, preferred_element_type=jnp.float32)
    return part * (1.0 / total), top * scale + jnp.log(total)


def fill_tables(n, tiles, sel, tblv):
    heads, entries = sel.shape
    each = entries // tiles
    picks = sel[...]
    lane = lax.broadcasted_iota(jnp.int32, (heads, entries), 1)
    tile_of = jnp.zeros((heads, entries), jnp.int32)
    for t in range(1, tiles):
        tile_of += jnp.where(lane >= t * each, 1, 0)
    other = lane != tile_of * each
    rank = jnp.zeros((heads, entries), jnp.int32)
    for j in range(entries):
        if j % each != 0:
            rank += jnp.where((picks == picks[:, j : j + 1]) & (lane > j) & other, 1, 0)
    slot = jnp.minimum(rank, CAP - 1)
    lanes = tblv.shape[2]
    wide = lax.broadcasted_iota(jnp.int32, (heads, lanes), 1)
    found = jnp.zeros((heads, lanes), jnp.int32)
    for a in range(n):
        for s in range(CAP):
            hit = other & (picks == a) & (slot == s)
            tile = jnp.max(jnp.where(hit, tile_of, 0), axis=1, keepdims=True)
            found = jnp.where(wide == a * CAP + s, tile, found)
    tblv[0] = found
    tblv[1] = jnp.zeros((heads, lanes), jnp.int32)
    tblv[2] = jnp.zeros((heads, lanes), jnp.int32)
    tblv[1, :, :entries] = picks
    tblv[2, :, :entries] = slot


def kernel(
    dims,
    sel,
    q_hbm,
    k_hbm,
    v_hbm,
    w_hbm,
    out_ref,
    q,
    k,
    v,
    w,
    qsend,
    osend,
    ssend,
    own,
    own_lse,
    att,
    acc,
    tblv,
    tbl,
    load_sem,
    qs_sem,
    qr_sem,
    os_sem,
    or_sem,
    ss_sem,
    sr_sem,
    as_sem,
    ar_sem,
    *grouped,
):
    n, nh, heads, tiles, rows, width, groups = dims
    per = heads // groups
    tokens = tiles * rows
    scale = width ** (-0.5)
    qrecv, orecv, srecv = (grouped[i * groups : (i + 1) * groups] for i in range(3))
    me = lax.axis_index("ctx")
    hd = lax.axis_index("head")

    loads = [
        pltpu.make_async_copy(src, dst, load_sem.at[i])
        for i, (src, dst) in enumerate(((q_hbm, q), (k_hbm, k), (v_hbm, v), (w_hbm, w)))
    ]
    for copy in loads:
        copy.start()

    barrier = pltpu.get_barrier_semaphore()

    def greet(d, _):
        pl.semaphore_signal(
            barrier, inc=1, device_id={"ctx": lax.rem(me + d, n)}, device_id_type=MESH
        )
        return 0

    lax.fori_loop(1, n, greet, 0)
    for j in range(1, nh):
        pl.semaphore_signal(
            barrier, inc=1, device_id={"head": lax.rem(hd + j, nh)}, device_id_type=MESH
        )

    def distance(i):
        half = (i + 1) // 2
        return n // 2 + jnp.where(i % 2 == 0, half, -half)

    def q_copy(g, there, here):
        return pltpu.make_async_remote_copy(
            src_ref=qsend.at[g, there],
            dst_ref=qrecv[g].at[here],
            send_sem=qs_sem.at[g, there],
            recv_sem=qr_sem.at[g, here],
            device_id={"ctx": there},
            device_id_type=MESH,
        )

    def o_copy(g, there, here):
        return pltpu.make_async_remote_copy(
            src_ref=osend.at[g, there],
            dst_ref=orecv[g].at[here],
            send_sem=os_sem.at[g, there],
            recv_sem=or_sem.at[g, here],
            device_id={"ctx": there},
            device_id_type=MESH,
        )

    def s_copy(g, there, here):
        return pltpu.make_async_remote_copy(
            src_ref=ssend.at[g, there],
            dst_ref=srecv[g].at[here],
            send_sem=ss_sem.at[g, there],
            recv_sem=sr_sem.at[g, here],
            device_id={"ctx": there},
            device_id_type=MESH,
        )

    def a_copy(g, there, here):
        return pltpu.make_async_remote_copy(
            src_ref=att.at[here, g],
            dst_ref=att.at[here, g],
            send_sem=as_sem.at[there, g],
            recv_sem=ar_sem.at[here, g],
            device_id={"head": there},
            device_id_type=MESH,
        )

    fill_tables(n, tiles, sel, tblv)
    to_scalars = pltpu.make_async_copy(tblv, tbl, load_sem.at[4])
    to_scalars.start()
    loads[0].wait()
    to_scalars.wait()
    pl.semaphore_wait(barrier, n - 1 + nh - 1)

    def send_group(g):
        def send_queries(i, _):
            there = me - distance(i)

            @pl.when(there >= 0)
            def _():
                for hh in range(per):
                    h = g * per + hh
                    for s in range(CAP):
                        tile = tbl[0, h, there * CAP + s]
                        qsend[g, there, hh, s] = q[tile, :, h * width : (h + 1) * width]
                q_copy(g, there, me).start()

            return 0

        lax.fori_loop(0, n - 1, send_queries, 0)

    for g in range(min(AHEAD, groups)):
        send_group(g)
    loads[1].wait()
    loads[2].wait()
    causal = lax.broadcasted_iota(jnp.int32, (tokens, tokens), 0) >= lax.broadcasted_iota(
        jnp.int32, (tokens, tokens), 1
    )
    for h in range(heads):
        cols = slice(h * width, (h + 1) * width)
        query = q[:, :, cols].reshape(tokens, width)
        part, lse = softmax_block(query, k[:, cols], v[:, cols], scale, causal)
        own[h] = part.reshape(tiles, rows, width)
        own_lse[h] = jnp.broadcast_to(lse, (tokens, width)).reshape(tiles, rows, width)

    short = CAP * rows
    stat_lanes = ssend.shape[3]
    lane = lax.broadcasted_iota(jnp.int32, (short, stat_lanes), 1)
    row = lax.broadcasted_iota(jnp.int32, (short, stat_lanes), 0)

    def answer_group(g):
        orecv[g][me] = jnp.zeros((per, CAP, rows, width), jnp.bfloat16)
        srecv[g][me] = jnp.full((1, stat_lanes), -1e30, jnp.float32)

        def answer(i, _):
            there = me + distance(i)

            @pl.when(there < n)
            def _():
                q_copy(g, me, there).wait_recv()
                stats = jnp.zeros((short, stat_lanes), jnp.float32)
                for hh in range(per):
                    h = g * per + hh
                    cols = slice(h * width, (h + 1) * width)
                    query = qrecv[g][there, hh].reshape(short, width)
                    part, lse = softmax_block(query, k[:, cols], v[:, cols], scale, None)
                    osend[g, there, hh] = part.astype(jnp.bfloat16).reshape(CAP, rows, width)
                    stats = jnp.where(lane == row + hh * short, lse, stats)
                ssend[g, there] = jnp.sum(stats, axis=0, keepdims=True)
                o_copy(g, there, me).start()
                s_copy(g, there, me).start()

            return 0

        lax.fori_loop(0, n - 1, answer, 0)

    part_cols = min(256, out_ref.shape[1])

    def project(p, g, first):
        def body(c, _):
            at = pl.ds(pl.multiple_of(c * part_cols, part_cols), part_cols)
            term = jnp.dot(att[p, g], w[p, g, :, at], preferred_element_type=jnp.float32)
            if first:
                acc[:, at] = term
            else:
                acc[:, at] += term
            return 0

        lax.fori_loop(0, out_ref.shape[1] // part_cols, body, 0)

    lane_tile = lax.broadcasted_iota(jnp.int32, (rows, stat_lanes), 1)
    lane_tile = lane_tile - lax.broadcasted_iota(jnp.int32, (rows, stat_lanes), 0)

    def collect_group(g):
        def collect(i, _):
            there = me - distance(i)

            @pl.when(there >= 0)
            def _():
                s_copy(g, me, there).wait_recv()
                o_copy(g, me, there).wait_recv()

            return 0

        lax.fori_loop(0, n - 1, collect, 0)

        def picked_lse(block, slot, hh):
            hit = lane_tile == hh * short + slot * rows
            return jnp.sum(jnp.where(hit, srecv[g][block], 0.0), axis=1, keepdims=True)

        def combine(t, _):
            for hh in range(per):
                h = g * per + hh
                a1, a2 = tbl[1, h, t * 3 + 1], tbl[1, h, t * 3 + 2]
                s1, s2 = tbl[2, h, t * 3 + 1], tbl[2, h, t * 3 + 2]
                l0 = own_lse[h, t]
                l1, l2 = picked_lse(a1, s1, hh), picked_lse(a2, s2, hh)
                top = jnp.maximum(l0, jnp.maximum(l1, l2))
                w0, w1, w2 = jnp.exp(l0 - top), jnp.exp(l1 - top), jnp.exp(l2 - top)
                o1 = orecv[g][a1, hh, s1].astype(jnp.float32)
                o2 = orecv[g][a2, hh, s2].astype(jnp.float32)
                mixed = (w0 * own[h, t] + w1 * o1 + w2 * o2) / (w0 + w1 + w2)
                at = pl.ds(pl.multiple_of(t * rows, rows), rows)
                att[hd, g, at, hh * width : (hh + 1) * width] = mixed.astype(jnp.bfloat16)
            return 0

        lax.fori_loop(0, tiles, combine, 0)
        for j in range(1, nh):
            a_copy(g, lax.rem(hd + j, nh), hd).start()

    for g in range(groups):
        answer_group(g)
        if g + AHEAD < groups:
            send_group(g + AHEAD)
        if g >= LAG:
            collect_group(g - LAG)
    for g in range(max(groups - LAG, 0), groups):
        collect_group(g)
    loads[3].wait()
    for g in range(groups):
        project(hd, g, g == 0)
    for g in range(groups):
        for j in range(1, nh):
            peer = lax.rem(hd + j, nh)
            a_copy(g, hd, peer).wait_recv()
            project(peer, g, False)
    out_ref[...] = acc[...].astype(out_ref.dtype)

    for g in range(groups):

        def drain(i, _, g=g):
            d = distance(i)

            @pl.when(me - d >= 0)
            def _():
                q_copy(g, me - d, me).wait_send()

            @pl.when(me + d < n)
            def _():
                o_copy(g, me + d, me).wait_send()
                s_copy(g, me + d, me).wait_send()

            return 0

        lax.fori_loop(0, n - 1, drain, 0)
        for j in range(1, nh):
            a_copy(g, lax.rem(hd + j, nh), hd).wait_send()


def solution(mesh):
    n, nh = mesh.shape["ctx"], mesh.shape["head"]

    def local(queries, keys, values, selected, out_weight):
        heads, tiles = selected.shape[:2]
        tokens, cols = queries.shape[0], out_weight.shape[1]
        width = queries.shape[1] // heads
        rows = tokens // tiles
        per = 2 if heads % 2 == 0 and heads >= 4 else 1
        groups = heads // per
        stat_lanes = -(-per * CAP * rows // 128) * 128
        table = (3, heads, -(-max(n * CAP, tiles * 3) // 128) * 128)
        bf16, f32 = jnp.bfloat16, jnp.float32
        dma = pltpu.SemaphoreType.DMA
        packet = (n, per, CAP, rows, width)
        grouped = (
            [pltpu.VMEM(packet, bf16)] * (2 * groups)
            + [pltpu.VMEM((n, 1, stat_lanes), f32)] * groups
        )
        weight = out_weight.reshape(nh, groups, per * width, cols)
        return pl.pallas_call(
            functools.partial(kernel, (n, nh, heads, tiles, rows, width, groups)),
            out_shape=jax.ShapeDtypeStruct((tokens, cols), bf16),
            in_specs=[pl.BlockSpec(memory_space=pltpu.VMEM)]
            + [pl.BlockSpec(memory_space=pl.ANY)] * 4,
            out_specs=pl.BlockSpec(memory_space=pltpu.VMEM),
            scratch_shapes=[
                pltpu.VMEM((tiles, rows, heads * width), bf16),
                pltpu.VMEM((tokens, heads * width), bf16),
                pltpu.VMEM((tokens, heads * width), bf16),
                pltpu.VMEM(weight.shape, bf16),
                pltpu.VMEM((groups,) + packet, bf16),
                pltpu.VMEM((groups,) + packet, bf16),
                pltpu.VMEM((groups, n, 1, stat_lanes), f32),
                pltpu.VMEM((heads, tiles, rows, width), f32),
                pltpu.VMEM((heads, tiles, rows, width), f32),
                pltpu.VMEM((nh, groups, tokens, per * width), bf16),
                pltpu.VMEM((tokens, cols), f32),
                pltpu.VMEM(table, jnp.int32),
                pltpu.SMEM(table, jnp.int32),
                dma((5,)),
                dma((groups, n)),
                dma((groups, n)),
                dma((groups, n)),
                dma((groups, n)),
                dma((groups, n)),
                dma((groups, n)),
                dma((nh, groups)),
                dma((nh, groups)),
            ]
            + grouped,
            compiler_params=pltpu.CompilerParams(
                collective_id=0, has_side_effects=True, vmem_limit_bytes=56 * 1024 * 1024
            ),
        )(
            selected.reshape(heads, -1),
            queries.reshape(tiles, rows, heads * width),
            keys,
            values,
            weight,
        )

    return jax.shard_map(
        local,
        mesh=mesh,
        in_specs=(
            P("ctx", "head"),
            P("ctx", "head"),
            P("ctx", "head"),
            P("head", "ctx", None),
            P(None, "head"),
        ),
        out_specs=P("ctx", "head"),
        check_vma=False,
    )
```

```python
import functools

import jax
import jax.numpy as jnp
from jax import lax
from jax.experimental import pallas as pl
from jax.experimental.pallas import tpu as pltpu
from jax.sharding import PartitionSpec as P

CAP = 2
AHEAD = 2
LAG = 2
TEAM = 4
MESH = pl.DeviceIdType.MESH
LOG2E = 1.4426950408889634
NT = (((1,), (1,)), ((), ()))


def softmax_block(query, key, value, scale, mask):
    scores = lax.dot_general(query, key, NT, preferred_element_type=jnp.float32)
    if mask is not None:
        scores = jnp.where(mask, scores, jnp.float32(-1e30))
    top = jnp.max(scores, axis=-1, keepdims=True)
    prob = jnp.exp2((scores - top) * (scale * LOG2E))
    total = jnp.sum(prob, axis=-1, keepdims=True)
    part = jnp.dot(prob.astype(jnp.bfloat16), value, preferred_element_type=jnp.float32)
    return part * (1.0 / total), top * scale + jnp.log(total)


def fill_tables(n, tiles, sel, tblv):
    heads, _, each = sel.shape
    entries = tiles * each
    lane = lax.broadcasted_iota(jnp.int32, (heads, entries), 1)
    picks = jnp.zeros((heads, entries), jnp.int32)
    column = []
    for t in range(tiles):
        chosen = sel[:, t, :]
        for r in range(each):
            column.append(chosen[:, r : r + 1])
            picks = jnp.where(lane == t * each + r, column[-1], picks)
    tile_of = jnp.zeros((heads, entries), jnp.int32)
    for t in range(1, tiles):
        tile_of += jnp.where(lane >= t * each, 1, 0)
    other = lane != tile_of * each
    rank = jnp.zeros((heads, entries), jnp.int32)
    for j in range(entries):
        if j % each != 0:
            rank += jnp.where((picks == column[j]) & (lane > j) & other, 1, 0)
    slot = jnp.minimum(rank, CAP - 1)
    lanes = tblv.shape[2]
    wide = lax.broadcasted_iota(jnp.int32, (heads, lanes), 1)
    found = jnp.zeros((heads, lanes), jnp.int32)
    for a in range(n):
        for s in range(CAP):
            hit = other & (picks == a) & (slot == s)
            tile = jnp.max(jnp.where(hit, tile_of, 0), axis=1, keepdims=True)
            found = jnp.where(wide == a * CAP + s, tile, found)
    tblv[0] = found
    tblv[1] = jnp.zeros((heads, lanes), jnp.int32)
    tblv[2] = jnp.zeros((heads, lanes), jnp.int32)
    tblv[1, :, :entries] = picks
    tblv[2, :, :entries] = slot


def kernel(
    dims,
    sel,
    q_hbm,
    k_hbm,
    v_hbm,
    w_hbm,
    out_ref,
    q,
    k,
    v,
    w,
    qsend,
    osend,
    ssend,
    own,
    own_lse,
    att,
    acc,
    tblv,
    tbl,
    load_sem,
    qs_sem,
    qr_sem,
    os_sem,
    or_sem,
    ss_sem,
    sr_sem,
    as_sem,
    ar_sem,
    *grouped,
):
    n, nh, heads, tiles, rows, width, groups = dims
    per = heads // groups
    tokens = tiles * rows
    scale = width ** (-0.5)
    qrecv, orecv, srecv = (grouped[i * groups : (i + 1) * groups] for i in range(3))
    me = lax.axis_index("ctx")
    hd = lax.axis_index("head")

    loads = [
        pltpu.make_async_copy(src, dst, load_sem.at[i])
        for i, (src, dst) in enumerate(((q_hbm, q), (k_hbm, k), (v_hbm, v), (w_hbm, w)))
    ]
    for copy in loads:
        copy.start()

    barrier = pltpu.get_barrier_semaphore()

    def greet(d, _):
        pl.semaphore_signal(
            barrier, inc=1, device_id={"ctx": lax.rem(me + d, n)}, device_id_type=MESH
        )
        return 0

    lax.fori_loop(1, n, greet, 0)
    for j in range(1, nh):
        pl.semaphore_signal(
            barrier, inc=1, device_id={"head": lax.rem(hd + j, nh)}, device_id_type=MESH
        )

    level, place = me // TEAM, lax.rem(me, TEAM)
    levels = n // TEAM

    def distance(i):
        half = (i + 1) // 2
        return levels // 2 + jnp.where(i % 2 == 0, half, -half)

    def member(at_level, j):
        return at_level * TEAM + lax.rem(place + j, TEAM)

    def q_copy(g, there, here):
        return pltpu.make_async_remote_copy(
            src_ref=qsend.at[g, there],
            dst_ref=qrecv[g].at[here],
            send_sem=qs_sem.at[g, there],
            recv_sem=qr_sem.at[g, here],
            device_id={"ctx": there},
            device_id_type=MESH,
        )

    def o_copy(g, there, here):
        return pltpu.make_async_remote_copy(
            src_ref=osend.at[g, there],
            dst_ref=orecv[g].at[here],
            send_sem=os_sem.at[g, there],
            recv_sem=or_sem.at[g, here],
            device_id={"ctx": there},
            device_id_type=MESH,
        )

    def s_copy(g, there, here):
        return pltpu.make_async_remote_copy(
            src_ref=ssend.at[g, there],
            dst_ref=srecv[g].at[here],
            send_sem=ss_sem.at[g, there],
            recv_sem=sr_sem.at[g, here],
            device_id={"ctx": there},
            device_id_type=MESH,
        )

    def a_copy(g, there, here):
        return pltpu.make_async_remote_copy(
            src_ref=att.at[here, g],
            dst_ref=att.at[here, g],
            send_sem=as_sem.at[there, g],
            recv_sem=ar_sem.at[here, g],
            device_id={"head": there},
            device_id_type=MESH,
        )

    fill_tables(n, tiles, sel, tblv)
    to_scalars = pltpu.make_async_copy(tblv, tbl, load_sem.at[4])
    to_scalars.start()
    loads[0].wait()
    to_scalars.wait()
    pl.semaphore_wait(barrier, n - 1 + nh - 1)

    def send_group(g):
        def send_queries(i, _):
            there = member(level - distance(i // TEAM), lax.rem(i, TEAM))

            @pl.when((there >= 0) & (there < me))
            def _():
                for hh in range(per):
                    h = g * per + hh
                    for s in range(CAP):
                        tile = tbl[0, h, there * CAP + s]
                        qsend[g, there, hh, s] = q[tile, :, h * width : (h + 1) * width]
                q_copy(g, there, me).start()

            return 0

        lax.fori_loop(0, n, send_queries, 0)

    for g in range(min(AHEAD, groups)):
        send_group(g)
    loads[1].wait()
    loads[2].wait()
    causal = lax.broadcasted_iota(jnp.int32, (tokens, tokens), 0) >= lax.broadcasted_iota(
        jnp.int32, (tokens, tokens), 1
    )
    for h in range(heads):
        cols = slice(h * width, (h + 1) * width)
        query = q[:, :, cols].reshape(tokens, width)
        part, lse = softmax_block(query, k[:, cols], v[:, cols], scale, causal)
        own[h] = part.reshape(tiles, rows, width)
        own_lse[h] = jnp.broadcast_to(lse, (tokens, width)).reshape(tiles, rows, width)

    short = CAP * rows
    stat_lanes = ssend.shape[3]
    lane = lax.broadcasted_iota(jnp.int32, (TEAM, short, stat_lanes), 2)
    lane = lane - lax.broadcasted_iota(jnp.int32, (TEAM, short, stat_lanes), 1)

    def answer_group(g):
        orecv[g][me] = jnp.zeros((per, CAP, rows, width), jnp.bfloat16)
        srecv[g][me] = jnp.full((1, stat_lanes), -1e30, jnp.float32)

        def answer(i, _):
            their = level + distance(i)

            @pl.when(their < levels)
            def _():
                for j in range(TEAM):
                    there = member(their, j)

                    @pl.when(there > me)
                    def _():
                        q_copy(g, me, there).wait_recv()

                team = pl.ds(pl.multiple_of(their * TEAM, TEAM), TEAM)
                stats = jnp.zeros((TEAM, short, stat_lanes), jnp.float32)
                for hh in range(per):
                    h = g * per + hh
                    cols = slice(h * width, (h + 1) * width)
                    query = qrecv[g][team, hh].reshape(TEAM * short, width)
                    part, lse = softmax_block(query, k[:, cols], v[:, cols], scale, None)
                    osend[g, team, hh] = part.astype(jnp.bfloat16).reshape(TEAM, CAP, rows, width)
                    lse = jnp.broadcast_to(lse, (TEAM * short, stat_lanes))
                    lse = lse.reshape(TEAM, short, stat_lanes)
                    stats = jnp.where(lane == hh * short, lse, stats)
                ssend[g, team] = jnp.sum(stats, axis=1, keepdims=True)
                for j in range(TEAM):
                    there = member(their, j)

                    @pl.when(there > me)
                    def _():
                        o_copy(g, there, me).start()
                        s_copy(g, there, me).start()

            return 0

        lax.fori_loop(0, levels, answer, 0)

    part_cols = min(256, out_ref.shape[1])

    def project(p, last):
        def body(c, _):
            at = pl.ds(pl.multiple_of(c * part_cols, part_cols), part_cols)
            term = 0.0 if p is hd else acc[:, at]
            for g in range(groups):
                term += jnp.dot(att[p, g], w[p, g, :, at], preferred_element_type=jnp.float32)
            if last:
                out_ref[:, at] = term.astype(out_ref.dtype)
            else:
                acc[:, at] = term
            return 0

        lax.fori_loop(0, out_ref.shape[1] // part_cols, body, 0)

    lane_tile = lax.broadcasted_iota(jnp.int32, (rows, stat_lanes), 1)
    lane_tile = lane_tile - lax.broadcasted_iota(jnp.int32, (rows, stat_lanes), 0)

    def collect_group(g):
        def collect(i, _):
            there = member(level - distance(i // TEAM), lax.rem(i, TEAM))

            @pl.when((there >= 0) & (there < me))
            def _():
                s_copy(g, me, there).wait_recv()
                o_copy(g, me, there).wait_recv()

            return 0

        lax.fori_loop(0, n, collect, 0)

        def picked_lse(block, slot, hh):
            hit = lane_tile == hh * short + slot * rows
            return jnp.sum(jnp.where(hit, srecv[g][block], 0.0), axis=1, keepdims=True)

        for hh in range(per):
            h = g * per + hh

            def gather(r):
                blocks = [tbl[1, h, t * 3 + r] for t in range(tiles)]
                slots = [tbl[2, h, t * 3 + r] for t in range(tiles)]
                outs = [orecv[g][a, hh, s] for a, s in zip(blocks, slots)]
                lses = [picked_lse(a, s, hh) for a, s in zip(blocks, slots)]
                return jnp.concatenate(outs, 0).astype(jnp.float32), jnp.concatenate(lses, 0)

            (o1, l1), (o2, l2) = gather(1), gather(2)
            l0 = own_lse[h].reshape(tokens, width)
            top = jnp.maximum(l0, jnp.maximum(l1, l2))
            w0, w1, w2 = jnp.exp(l0 - top), jnp.exp(l1 - top), jnp.exp(l2 - top)
            mixed = w0 * own[h].reshape(tokens, width) + w1 * o1 + w2 * o2
            mixed = mixed / (w0 + w1 + w2)
            att[hd, g, :, hh * width : (hh + 1) * width] = mixed.astype(jnp.bfloat16)
        for j in range(1, nh):
            a_copy(g, lax.rem(hd + j, nh), hd).start()

    for g in range(groups):
        answer_group(g)
        if g + AHEAD < groups:
            send_group(g + AHEAD)
        if g >= LAG:
            collect_group(g - LAG)
    for g in range(max(groups - LAG, 0), groups):
        collect_group(g)
    loads[3].wait()
    project(hd, nh == 1)
    for j in range(1, nh):
        peer = lax.rem(hd + j, nh)
        for g in range(groups):
            a_copy(g, hd, peer).wait_recv()
        project(peer, j == nh - 1)

    for g in range(groups):

        def drain(d, _, g=g):
            @pl.when(me - d >= 0)
            def _():
                q_copy(g, me - d, me).wait_send()

            @pl.when(me + d < n)
            def _():
                o_copy(g, me + d, me).wait_send()
                s_copy(g, me + d, me).wait_send()

            return 0

        lax.fori_loop(1, n, drain, 0)
        for j in range(1, nh):
            a_copy(g, lax.rem(hd + j, nh), hd).wait_send()


def solution(mesh):
    n, nh = mesh.shape["ctx"], mesh.shape["head"]

    def local(queries, keys, values, selected, out_weight):
        heads, tiles = selected.shape[:2]
        tokens, cols = queries.shape[0], out_weight.shape[1]
        width = queries.shape[1] // heads
        rows = tokens // tiles
        per = 2 if heads % 2 == 0 and heads >= 4 else 1
        groups = heads // per
        stat_lanes = -(-per * CAP * rows // 128) * 128
        table = (3, heads, -(-max(n * CAP, tiles * 3) // 128) * 128)
        bf16, f32 = jnp.bfloat16, jnp.float32
        dma = pltpu.SemaphoreType.DMA
        packet = (n, per, CAP, rows, width)
        grouped = (
            [pltpu.VMEM(packet, bf16)] * (2 * groups)
            + [pltpu.VMEM((n, 1, stat_lanes), f32)] * groups
        )
        weight = out_weight.reshape(nh, groups, per * width, cols)
        return pl.pallas_call(
            functools.partial(kernel, (n, nh, heads, tiles, rows, width, groups)),
            out_shape=jax.ShapeDtypeStruct((tokens, cols), bf16),
            in_specs=[pl.BlockSpec(memory_space=pltpu.VMEM)]
            + [pl.BlockSpec(memory_space=pl.ANY)] * 4,
            out_specs=pl.BlockSpec(memory_space=pltpu.VMEM),
            scratch_shapes=[
                pltpu.VMEM((tiles, rows, heads * width), bf16),
                pltpu.VMEM((tokens, heads * width), bf16),
                pltpu.VMEM((tokens, heads * width), bf16),
                pltpu.VMEM(weight.shape, bf16),
                pltpu.VMEM((groups,) + packet, bf16),
                pltpu.VMEM((groups,) + packet, bf16),
                pltpu.VMEM((groups, n, 1, stat_lanes), f32),
                pltpu.VMEM((heads, tiles, rows, width), f32),
                pltpu.VMEM((heads, tiles, rows, width), f32),
                pltpu.VMEM((nh, groups, tokens, per * width), bf16),
                pltpu.VMEM((tokens, cols), f32),
                pltpu.VMEM(table, jnp.int32),
                pltpu.SMEM(table, jnp.int32),
                dma((5,)),
                dma((groups, n)),
                dma((groups, n)),
                dma((groups, n)),
                dma((groups, n)),
                dma((groups, n)),
                dma((groups, n)),
                dma((nh, groups)),
                dma((nh, groups)),
            ]
            + grouped,
            compiler_params=pltpu.CompilerParams(
                collective_id=0, has_side_effects=True, vmem_limit_bytes=56 * 1024 * 1024
            ),
        )(
            selected,
            queries.reshape(tiles, rows, heads * width),
            keys,
            values,
            weight,
        )

    return jax.shard_map(
        local,
        mesh=mesh,
        in_specs=(
            P("ctx", "head"),
            P("ctx", "head"),
            P("ctx", "head"),
            P("head", "ctx", None),
            P(None, "head"),
        ),
        out_specs=P("ctx", "head"),
        check_vma=False,
    )
```

```python
import functools

import jax
import jax.numpy as jnp
from jax import lax
from jax.experimental import pallas as pl
from jax.experimental.pallas import tpu as pltpu
from jax.sharding import PartitionSpec as P

CAP = 2
AHEAD = 4
LAG = 2
TEAM = 4
MESH = pl.DeviceIdType.MESH
LOG2E = 1.4426950408889634
NT = (((1,), (1,)), ((), ()))


def softmax_block(query, key, value, scale, mask):
    scores = lax.dot_general(query, key, NT, preferred_element_type=jnp.float32)
    if mask is not None:
        scores = jnp.where(mask, scores, jnp.float32(-1e30))
    top = jnp.max(scores, axis=-1, keepdims=True)
    prob = jnp.exp2((scores - top) * (scale * LOG2E))
    total = jnp.sum(prob, axis=-1, keepdims=True)
    part = jnp.dot(prob.astype(jnp.bfloat16), value, preferred_element_type=jnp.float32)
    return part * (1.0 / total), top * scale + jnp.log(total)


def fill_tables(n, tiles, sel, tblv):
    each, heads, _ = sel.shape
    entries = (each - 1) * tiles
    lane = lax.broadcasted_iota(jnp.int32, (heads, entries), 1)
    picks = jnp.zeros((heads, entries), jnp.int32)
    tile_of = lane
    column = []
    for r in range(1, each):
        chosen = sel[r]
        tile_of = jnp.where(lane >= (r - 1) * tiles, lane - (r - 1) * tiles, tile_of)
        for t in range(tiles):
            column.append(chosen[:, t : t + 1])
            picks = jnp.where(lane == (r - 1) * tiles + t, column[-1], picks)
    rank = jnp.zeros((heads, entries), jnp.int32)
    for j in range(entries):
        rank += jnp.where((picks == column[j]) & (lane > j), 1, 0)
    slot = jnp.minimum(rank, CAP - 1)
    lanes = tblv.shape[2]
    wide = lax.broadcasted_iota(jnp.int32, (heads, lanes), 1)
    found = jnp.zeros((heads, lanes), jnp.int32)
    for a in range(n):
        for s in range(CAP):
            hit = (picks == a) & (slot == s)
            tile = jnp.max(jnp.where(hit, tile_of, 0), axis=1, keepdims=True)
            found = jnp.where(wide == a * CAP + s, tile, found)
    tblv[0] = found
    tblv[1] = jnp.zeros((heads, lanes), jnp.int32)
    tblv[2] = jnp.zeros((heads, lanes), jnp.int32)
    tblv[1, :, :entries] = picks
    tblv[2, :, :entries] = slot


def kernel(
    dims,
    sel,
    q_hbm,
    k_hbm,
    v_hbm,
    w_hbm,
    out_ref,
    q,
    k,
    v,
    w,
    qsend,
    osend,
    ssend,
    own,
    own_lse,
    att,
    acc,
    tblv,
    tbl,
    load_sem,
    qs_sem,
    qr_sem,
    os_sem,
    or_sem,
    ss_sem,
    sr_sem,
    as_sem,
    ar_sem,
    *grouped,
):
    n, nh, heads, tiles, rows, width, groups = dims
    per = heads // groups
    tokens = tiles * rows
    scale = width ** (-0.5)
    qrecv, orecv, srecv = (grouped[i * groups : (i + 1) * groups] for i in range(3))
    me = lax.axis_index("ctx")
    hd = lax.axis_index("head")

    loads = [
        pltpu.make_async_copy(src, dst, load_sem.at[i])
        for i, (src, dst) in enumerate(((q_hbm, q), (k_hbm, k), (v_hbm, v), (w_hbm, w)))
    ]
    for copy in loads:
        copy.start()

    barrier = pltpu.get_barrier_semaphore()

    def greet(d, _):
        pl.semaphore_signal(
            barrier, inc=1, device_id={"ctx": lax.rem(me + d, n)}, device_id_type=MESH
        )
        return 0

    lax.fori_loop(1, n, greet, 0)
    for j in range(1, nh):
        pl.semaphore_signal(
            barrier, inc=1, device_id={"head": lax.rem(hd + j, nh)}, device_id_type=MESH
        )

    level, place = me // TEAM, lax.rem(me, TEAM)
    levels = n // TEAM

    def distance(i):
        half = (i + 1) // 2
        return levels // 2 + jnp.where(i % 2 == 0, half, -half)

    def member(at_level, j):
        return at_level * TEAM + lax.rem(place + j, TEAM)

    def q_copy(g, there, here):
        return pltpu.make_async_remote_copy(
            src_ref=qsend.at[g, there],
            dst_ref=qrecv[g].at[here],
            send_sem=qs_sem.at[g, there],
            recv_sem=qr_sem.at[g, here],
            device_id={"ctx": there},
            device_id_type=MESH,
        )

    def o_copy(g, there, here):
        return pltpu.make_async_remote_copy(
            src_ref=osend.at[g, there],
            dst_ref=orecv[g].at[here],
            send_sem=os_sem.at[g, there],
            recv_sem=or_sem.at[g, here],
            device_id={"ctx": there},
            device_id_type=MESH,
        )

    def s_copy(g, there, here):
        return pltpu.make_async_remote_copy(
            src_ref=ssend.at[g, there],
            dst_ref=srecv[g].at[here],
            send_sem=ss_sem.at[g, there],
            recv_sem=sr_sem.at[g, here],
            device_id={"ctx": there},
            device_id_type=MESH,
        )

    def a_copy(g, there, here):
        return pltpu.make_async_remote_copy(
            src_ref=att.at[here, g],
            dst_ref=att.at[here, g],
            send_sem=as_sem.at[there, g],
            recv_sem=ar_sem.at[here, g],
            device_id={"head": there},
            device_id_type=MESH,
        )

    fill_tables(n, tiles, sel, tblv)
    to_scalars = pltpu.make_async_copy(tblv, tbl, load_sem.at[4])
    to_scalars.start()
    loads[0].wait()
    to_scalars.wait()
    pl.semaphore_wait(barrier, n - 1 + nh - 1)

    def send_group(g):
        def send_queries(i, _):
            there = member(level - distance(i // TEAM), lax.rem(i, TEAM))

            @pl.when((there >= 0) & (there < me))
            def _():
                for hh in range(per):
                    h = g * per + hh
                    for s in range(CAP):
                        tile = tbl[0, h, there * CAP + s]
                        qsend[g, there, hh, s] = q[tile, :, h * width : (h + 1) * width]
                q_copy(g, there, me).start()

            return 0

        lax.fori_loop(0, n, send_queries, 0)

    for g in range(min(AHEAD, groups)):
        send_group(g)
    loads[1].wait()
    loads[2].wait()
    causal = lax.broadcasted_iota(jnp.int32, (tokens, tokens), 0) >= lax.broadcasted_iota(
        jnp.int32, (tokens, tokens), 1
    )
    def own_group(g):
        for h in range(g * per, (g + 1) * per):
            cols = slice(h * width, (h + 1) * width)
            query = q[:, :, cols].reshape(tokens, width)
            part, lse = softmax_block(query, k[:, cols], v[:, cols], scale, causal)
            own[h] = part.reshape(tiles, rows, width)
            own_lse[h] = jnp.broadcast_to(lse, (tokens, width)).reshape(tiles, rows, width)

    short = CAP * rows
    stat_lanes = ssend.shape[3]
    lane = lax.broadcasted_iota(jnp.int32, (TEAM, short, stat_lanes), 2)
    lane = lane - lax.broadcasted_iota(jnp.int32, (TEAM, short, stat_lanes), 1)

    def answer_group(g):
        orecv[g][me] = jnp.zeros((per, CAP, rows, width), jnp.bfloat16)
        srecv[g][me] = jnp.full((1, stat_lanes), -1e30, jnp.float32)

        def answer(i, _):
            their = level + distance(i)

            @pl.when(their < levels)
            def _():
                for j in range(TEAM):
                    there = member(their, j)

                    @pl.when(there > me)
                    def _():
                        q_copy(g, me, there).wait_recv()

                team = pl.ds(pl.multiple_of(their * TEAM, TEAM), TEAM)
                stats = jnp.zeros((TEAM, short, stat_lanes), jnp.float32)
                for hh in range(per):
                    h = g * per + hh
                    cols = slice(h * width, (h + 1) * width)
                    query = qrecv[g][team, hh].reshape(TEAM * short, width)
                    part, lse = softmax_block(query, k[:, cols], v[:, cols], scale, None)
                    osend[g, team, hh] = part.astype(jnp.bfloat16).reshape(TEAM, CAP, rows, width)
                    lse = jnp.broadcast_to(lse, (TEAM * short, stat_lanes))
                    lse = lse.reshape(TEAM, short, stat_lanes)
                    stats = jnp.where(lane == hh * short, lse, stats)
                ssend[g, team] = jnp.sum(stats, axis=1, keepdims=True)
                for j in range(TEAM):
                    there = member(their, j)

                    @pl.when(there > me)
                    def _():
                        o_copy(g, there, me).start()
                        s_copy(g, there, me).start()

            return 0

        lax.fori_loop(0, levels, answer, 0)

    part_cols = min(256, out_ref.shape[1])

    def project(p, last):
        def body(c, _):
            at = pl.ds(pl.multiple_of(c * part_cols, part_cols), part_cols)
            term = 0.0 if p is hd else acc[:, at]
            for g in range(groups):
                term += jnp.dot(att[p, g], w[p, g, :, at], preferred_element_type=jnp.float32)
            if last:
                out_ref[:, at] = term.astype(out_ref.dtype)
            else:
                acc[:, at] = term
            return 0

        lax.fori_loop(0, out_ref.shape[1] // part_cols, body, 0)

    lane_tile = lax.broadcasted_iota(jnp.int32, (rows, stat_lanes), 1)
    lane_tile = lane_tile - lax.broadcasted_iota(jnp.int32, (rows, stat_lanes), 0)

    def collect_group(g):
        def collect(i, _):
            there = member(level - distance(i // TEAM), lax.rem(i, TEAM))

            @pl.when((there >= 0) & (there < me))
            def _():
                s_copy(g, me, there).wait_recv()
                o_copy(g, me, there).wait_recv()

            return 0

        lax.fori_loop(0, n, collect, 0)

        def picked_lse(block, slot, hh):
            hit = lane_tile == hh * short + slot * rows
            return jnp.sum(jnp.where(hit, srecv[g][block], 0.0), axis=1, keepdims=True)

        for hh in range(per):
            h = g * per + hh

            def gather(r):
                blocks = [tbl[1, h, (r - 1) * tiles + t] for t in range(tiles)]
                slots = [tbl[2, h, (r - 1) * tiles + t] for t in range(tiles)]
                outs = [orecv[g][a, hh, s] for a, s in zip(blocks, slots)]
                lses = [picked_lse(a, s, hh) for a, s in zip(blocks, slots)]
                return jnp.concatenate(outs, 0).astype(jnp.float32), jnp.concatenate(lses, 0)

            (o1, l1), (o2, l2) = gather(1), gather(2)
            l0 = own_lse[h].reshape(tokens, width)
            top = jnp.maximum(l0, jnp.maximum(l1, l2))
            w0, w1, w2 = jnp.exp(l0 - top), jnp.exp(l1 - top), jnp.exp(l2 - top)
            mixed = w0 * own[h].reshape(tokens, width) + w1 * o1 + w2 * o2
            mixed = mixed / (w0 + w1 + w2)
            att[hd, g, :, hh * width : (hh + 1) * width] = mixed.astype(jnp.bfloat16)
        for j in range(1, nh):
            a_copy(g, lax.rem(hd + j, nh), hd).start()

    own_group(0)
    for g in range(groups):
        answer_group(g)
        if g + AHEAD < groups:
            send_group(g + AHEAD)
        if g + 1 < groups:
            own_group(g + 1)
        if g >= LAG:
            collect_group(g - LAG)
    for g in range(max(groups - LAG, 0), groups):
        collect_group(g)
    loads[3].wait()
    project(hd, nh == 1)
    for j in range(1, nh):
        peer = lax.rem(hd + j, nh)
        for g in range(groups):
            a_copy(g, hd, peer).wait_recv()
        project(peer, j == nh - 1)

    for g in range(groups):

        def drain(d, _, g=g):
            @pl.when(me - d >= 0)
            def _():
                q_copy(g, me - d, me).wait_send()

            @pl.when(me + d < n)
            def _():
                o_copy(g, me + d, me).wait_send()
                s_copy(g, me + d, me).wait_send()

            return 0

        lax.fori_loop(1, n, drain, 0)
        for j in range(1, nh):
            a_copy(g, lax.rem(hd + j, nh), hd).wait_send()


def solution(mesh):
    n, nh = mesh.shape["ctx"], mesh.shape["head"]

    def local(queries, keys, values, selected, out_weight):
        heads, tiles = selected.shape[:2]
        tokens, cols = queries.shape[0], out_weight.shape[1]
        width = queries.shape[1] // heads
        rows = tokens // tiles
        per = 2 if heads % 2 == 0 and heads >= 4 else 1
        groups = heads // per
        stat_lanes = -(-per * CAP * rows // 128) * 128
        table = (3, heads, -(-max(n * CAP, tiles * 3) // 128) * 128)
        bf16, f32 = jnp.bfloat16, jnp.float32
        dma = pltpu.SemaphoreType.DMA
        packet = (n, per, CAP, rows, width)
        grouped = (
            [pltpu.VMEM(packet, bf16)] * (2 * groups)
            + [pltpu.VMEM((n, 1, stat_lanes), f32)] * groups
        )
        weight = out_weight.reshape(nh, groups, per * width, cols)
        return pl.pallas_call(
            functools.partial(kernel, (n, nh, heads, tiles, rows, width, groups)),
            out_shape=jax.ShapeDtypeStruct((tokens, cols), bf16),
            in_specs=[pl.BlockSpec(memory_space=pltpu.VMEM)]
            + [pl.BlockSpec(memory_space=pl.ANY)] * 4,
            out_specs=pl.BlockSpec(memory_space=pltpu.VMEM),
            scratch_shapes=[
                pltpu.VMEM((tiles, rows, heads * width), bf16),
                pltpu.VMEM((tokens, heads * width), bf16),
                pltpu.VMEM((tokens, heads * width), bf16),
                pltpu.VMEM(weight.shape, bf16),
                pltpu.VMEM((groups,) + packet, bf16),
                pltpu.VMEM((groups,) + packet, bf16),
                pltpu.VMEM((groups, n, 1, stat_lanes), f32),
                pltpu.VMEM((heads, tiles, rows, width), f32),
                pltpu.VMEM((heads, tiles, rows, width), f32),
                pltpu.VMEM((nh, groups, tokens, per * width), bf16),
                pltpu.VMEM((tokens, cols), f32),
                pltpu.VMEM(table, jnp.int32),
                pltpu.SMEM(table, jnp.int32),
                dma((5,)),
                dma((groups, n)),
                dma((groups, n)),
                dma((groups, n)),
                dma((groups, n)),
                dma((groups, n)),
                dma((groups, n)),
                dma((nh, groups)),
                dma((nh, groups)),
            ]
            + grouped,
            compiler_params=pltpu.CompilerParams(
                collective_id=0, has_side_effects=True, vmem_limit_bytes=56 * 1024 * 1024
            ),
        )(
            jnp.transpose(selected, (2, 0, 1)),
            queries.reshape(tiles, rows, heads * width),
            keys,
            values,
            weight,
        )

    return jax.shard_map(
        local,
        mesh=mesh,
        in_specs=(
            P("ctx", "head"),
            P("ctx", "head"),
            P("ctx", "head"),
            P("head", "ctx", None),
            P(None, "head"),
        ),
        out_specs=P("ctx", "head"),
        check_vma=False,
    )
```

```python
import functools

import jax
import jax.numpy as jnp
from jax import lax
from jax.experimental import pallas as pl
from jax.experimental.pallas import tpu as pltpu
from jax.sharding import PartitionSpec as P

CAP = 2
AHEAD = 2
LAG = 1
TEAM = 4
MESH = pl.DeviceIdType.MESH
LOG2E = 1.4426950408889634
NT = (((1,), (1,)), ((), ()))


def softmax_block(query, key, value, scale, mask):
    scores = lax.dot_general(query, key, NT, preferred_element_type=jnp.float32)
    if mask is not None:
        scores = jnp.where(mask, scores, jnp.float32(-1e30))
    top = jnp.max(scores, axis=-1, keepdims=True)
    prob = jnp.exp2((scores - top) * (scale * LOG2E))
    total = jnp.sum(prob, axis=-1, keepdims=True)
    part = jnp.dot(prob.astype(jnp.bfloat16), value, preferred_element_type=jnp.float32)
    return part * (1.0 / total), top, total


def fill_tables(n, tiles, sel, tblv):
    each, heads, _ = sel.shape
    entries = (each - 1) * tiles
    lane = lax.broadcasted_iota(jnp.int32, (heads, entries), 1)
    picks = jnp.zeros((heads, entries), jnp.int32)
    tile_of = lane
    column = []
    for r in range(1, each):
        chosen = sel[r]
        tile_of = jnp.where(lane >= (r - 1) * tiles, lane - (r - 1) * tiles, tile_of)
        for t in range(tiles):
            column.append(chosen[:, t : t + 1])
            picks = jnp.where(lane == (r - 1) * tiles + t, column[-1], picks)
    rank = jnp.zeros((heads, entries), jnp.int32)
    for j in range(entries):
        rank += jnp.where((picks == column[j]) & (lane > j), 1, 0)
    slot = jnp.minimum(rank, CAP - 1)
    lanes = tblv.shape[2]
    wide = lax.broadcasted_iota(jnp.int32, (heads, lanes), 1)
    found = jnp.zeros((heads, lanes), jnp.int32)
    for a in range(n):
        for s in range(CAP):
            hit = (picks == a) & (slot == s)
            tile = jnp.max(jnp.where(hit, tile_of, 0), axis=1, keepdims=True)
            found = jnp.where(wide == a * CAP + s, tile, found)
    tblv[0] = found
    tblv[1] = jnp.zeros((heads, lanes), jnp.int32)
    tblv[2] = jnp.zeros((heads, lanes), jnp.int32)
    tblv[1, :, :entries] = picks
    tblv[2, :, :entries] = slot


def kernel(
    dims,
    sel,
    q_hbm,
    k_hbm,
    v_hbm,
    w_hbm,
    out_ref,
    q,
    k,
    v,
    w,
    qsend,
    osend,
    ssend,
    own,
    own_lse,
    att,
    acc,
    tblv,
    tbl,
    load_sem,
    qs_sem,
    qr_sem,
    os_sem,
    or_sem,
    ss_sem,
    sr_sem,
    as_sem,
    ar_sem,
    *grouped,
):
    n, nh, heads, tiles, rows, width, groups = dims
    per = heads // groups
    tokens = tiles * rows
    scale = width ** (-0.5)
    qrecv, orecv, srecv = (grouped[i * groups : (i + 1) * groups] for i in range(3))
    me = lax.axis_index("ctx")
    hd = lax.axis_index("head")

    loads = [
        pltpu.make_async_copy(src, dst, load_sem.at[i])
        for i, (src, dst) in enumerate(((q_hbm, q), (k_hbm, k), (v_hbm, v), (w_hbm, w)))
    ]
    for copy in loads:
        copy.start()

    barrier = pltpu.get_barrier_semaphore()

    def greet(d, _):
        pl.semaphore_signal(
            barrier, inc=1, device_id={"ctx": lax.rem(me + d, n)}, device_id_type=MESH
        )
        return 0

    lax.fori_loop(1, n, greet, 0)
    for j in range(1, nh):
        pl.semaphore_signal(
            barrier, inc=1, device_id={"head": lax.rem(hd + j, nh)}, device_id_type=MESH
        )

    level, place = me // TEAM, lax.rem(me, TEAM)
    levels = n // TEAM

    def distance(i):
        half = (i + 1) // 2
        return levels // 2 + jnp.where(i % 2 == 0, half, -half)

    def member(at_level, j):
        return at_level * TEAM + lax.rem(place + j, TEAM)

    def q_copy(g, there, here):
        return pltpu.make_async_remote_copy(
            src_ref=qsend.at[g, there],
            dst_ref=qrecv[g].at[here],
            send_sem=qs_sem.at[g, there],
            recv_sem=qr_sem.at[g, here],
            device_id={"ctx": there},
            device_id_type=MESH,
        )

    def o_copy(g, there, here):
        return pltpu.make_async_remote_copy(
            src_ref=osend.at[g, there],
            dst_ref=orecv[g].at[here],
            send_sem=os_sem.at[g, there],
            recv_sem=or_sem.at[g, here],
            device_id={"ctx": there},
            device_id_type=MESH,
        )

    def s_copy(g, there, here):
        return pltpu.make_async_remote_copy(
            src_ref=ssend.at[g, there],
            dst_ref=srecv[g].at[here],
            send_sem=ss_sem.at[g, there],
            recv_sem=sr_sem.at[g, here],
            device_id={"ctx": there},
            device_id_type=MESH,
        )

    def a_copy(g, there, here):
        return pltpu.make_async_remote_copy(
            src_ref=att.at[here, g],
            dst_ref=att.at[here, g],
            send_sem=as_sem.at[there, g],
            recv_sem=ar_sem.at[here, g],
            device_id={"head": there},
            device_id_type=MESH,
        )

    fill_tables(n, tiles, sel, tblv)
    to_scalars = pltpu.make_async_copy(tblv, tbl, load_sem.at[4])
    to_scalars.start()
    loads[0].wait()
    to_scalars.wait()
    pl.semaphore_wait(barrier, n - 1 + nh - 1)

    def send_group(g):
        def send_queries(i, _):
            there = member(level - distance(i // TEAM), lax.rem(i, TEAM))

            @pl.when((there >= 0) & (there < me))
            def _():
                for hh in range(per):
                    h = g * per + hh
                    for s in range(CAP):
                        tile = tbl[0, h, there * CAP + s]
                        qsend[g, there, hh, s] = q[tile, :, h * width : (h + 1) * width]
                q_copy(g, there, me).start()

            return 0

        lax.fori_loop(0, n, send_queries, 0)

    for g in range(min(AHEAD, groups)):
        send_group(g)
    loads[1].wait()
    loads[2].wait()
    causal = lax.broadcasted_iota(jnp.int32, (tokens, tokens), 0) >= lax.broadcasted_iota(
        jnp.int32, (tokens, tokens), 1
    )
    def own_group(g):
        for h in range(g * per, (g + 1) * per):
            cols = slice(h * width, (h + 1) * width)
            query = q[:, :, cols].reshape(tokens, width)
            part, top, total = softmax_block(query, k[:, cols], v[:, cols], scale, causal)
            lse = top * scale + jnp.log(total)
            own[h] = part.reshape(tiles, rows, width)
            own_lse[h] = jnp.broadcast_to(lse, (tokens, width)).reshape(tiles, rows, width)

    short = CAP * rows
    stat_lanes = ssend.shape[3]
    lane = lax.broadcasted_iota(jnp.int32, (TEAM, short, 128), 2)
    lane = lane - lax.broadcasted_iota(jnp.int32, (TEAM, short, 128), 1)

    def as_row(hit, column):
        column = jnp.broadcast_to(column, (TEAM * short, 128)).reshape(TEAM, short, 128)
        return jnp.sum(jnp.where(hit, column, 0.0), axis=1, keepdims=True)

    def answer_group(g):
        orecv[g][me] = jnp.zeros((per, CAP, rows, width), jnp.bfloat16)
        srecv[g][me] = jnp.full((1, stat_lanes), -1e30, jnp.float32)

        def answer(i, _):
            their = level + distance(i)

            @pl.when(their < levels)
            def _():
                for j in range(TEAM):
                    there = member(their, j)

                    @pl.when(there > me)
                    def _():
                        q_copy(g, me, there).wait_recv()

                team = pl.ds(pl.multiple_of(their * TEAM, TEAM), TEAM)
                both = 128 // short
                for first in range(0, per, both):
                    tops = jnp.zeros((TEAM, 1, 128), jnp.float32)
                    totals = jnp.zeros((TEAM, 1, 128), jnp.float32)
                    for hh in range(first, min(first + both, per)):
                        h = g * per + hh
                        cols = slice(h * width, (h + 1) * width)
                        query = qrecv[g][team, hh].reshape(TEAM * short, width)
                        part, top, total = softmax_block(query, k[:, cols], v[:, cols], scale, None)
                        part = part.astype(jnp.bfloat16).reshape(TEAM, CAP, rows, width)
                        osend[g, team, hh] = part
                        hit = lane == (hh - first) * short
                        tops += as_row(hit, top)
                        totals += as_row(hit, total)
                    ssend[g, team, :, first * short : first * short + 128] = tops * scale + jnp.log(
                        totals
                    )
                for j in range(TEAM):
                    there = member(their, j)

                    @pl.when(there > me)
                    def _():
                        o_copy(g, there, me).start()
                        s_copy(g, there, me).start()

            return 0

        lax.fori_loop(0, levels, answer, 0)

    part_cols = min(256, out_ref.shape[1])

    def project(p, last):
        def body(c, _):
            at = pl.ds(pl.multiple_of(c * part_cols, part_cols), part_cols)
            term = 0.0 if p is hd else acc[:, at]
            for g in range(groups):
                term += jnp.dot(att[p, g], w[p, g, :, at], preferred_element_type=jnp.float32)
            if last:
                out_ref[:, at] = term.astype(out_ref.dtype)
            else:
                acc[:, at] = term
            return 0

        lax.fori_loop(0, out_ref.shape[1] // part_cols, body, 0)

    lane_tile = lax.broadcasted_iota(jnp.int32, (rows, 128), 1)
    lane_tile = lane_tile - lax.broadcasted_iota(jnp.int32, (rows, 128), 0)

    def collect_group(g):
        def collect(i, _):
            there = member(level - distance(i // TEAM), lax.rem(i, TEAM))

            @pl.when((there >= 0) & (there < me))
            def _():
                s_copy(g, me, there).wait_recv()
                o_copy(g, me, there).wait_recv()

            return 0

        lax.fori_loop(0, n, collect, 0)

        def picked_lse(block, slot, hh):
            at = hh * short // 128 * 128
            hit = lane_tile == hh * short - at + slot * rows
            row = srecv[g][block][:, at : at + 128]
            return jnp.sum(jnp.where(hit, row, 0.0), axis=1, keepdims=True)

        for hh in range(per):
            h = g * per + hh

            def gather(r):
                blocks = [tbl[1, h, (r - 1) * tiles + t] for t in range(tiles)]
                slots = [tbl[2, h, (r - 1) * tiles + t] for t in range(tiles)]
                outs = [orecv[g][a, hh, s] for a, s in zip(blocks, slots)]
                lses = [picked_lse(a, s, hh) for a, s in zip(blocks, slots)]
                return jnp.concatenate(outs, 0).astype(jnp.float32), jnp.concatenate(lses, 0)

            (o1, l1), (o2, l2) = gather(1), gather(2)
            l0 = own_lse[h].reshape(tokens, width)
            top = jnp.maximum(l0, jnp.maximum(l1, l2))
            w0, w1, w2 = jnp.exp(l0 - top), jnp.exp(l1 - top), jnp.exp(l2 - top)
            mixed = w0 * own[h].reshape(tokens, width) + w1 * o1 + w2 * o2
            mixed = mixed / (w0 + w1 + w2)
            att[hd, g, :, hh * width : (hh + 1) * width] = mixed.astype(jnp.bfloat16)
        for j in range(1, nh):
            a_copy(g, lax.rem(hd + j, nh), hd).start()

    own_group(0)
    for g in range(groups):
        answer_group(g)
        if g + AHEAD < groups:
            send_group(g + AHEAD)
        if g + 1 < groups:
            own_group(g + 1)
        if g >= LAG:
            collect_group(g - LAG)
    for g in range(max(groups - LAG, 0), groups):
        collect_group(g)
    loads[3].wait()
    project(hd, nh == 1)
    for g in range(groups):

        def drain(d, _, g=g):
            @pl.when(me - d >= 0)
            def _():
                q_copy(g, me - d, me).wait_send()

            @pl.when(me + d < n)
            def _():
                o_copy(g, me + d, me).wait_send()
                s_copy(g, me + d, me).wait_send()

            return 0

        lax.fori_loop(1, n, drain, 0)

    for j in range(1, nh):
        peer = lax.rem(hd + j, nh)
        for g in range(groups):
            a_copy(g, hd, peer).wait_recv()
        project(peer, j == nh - 1)

    for g in range(groups):
        for j in range(1, nh):
            a_copy(g, lax.rem(hd + j, nh), hd).wait_send()


def solution(mesh):
    n, nh = mesh.shape["ctx"], mesh.shape["head"]

    def local(queries, keys, values, selected, out_weight):
        heads, tiles = selected.shape[:2]
        tokens, cols = queries.shape[0], out_weight.shape[1]
        width = queries.shape[1] // heads
        rows = tokens // tiles
        per = 4 if heads % 4 == 0 else 1
        groups = heads // per
        stat_lanes = -(-per * CAP * rows // 128) * 128
        table = (3, heads, -(-max(n * CAP, tiles * 3) // 128) * 128)
        bf16, f32 = jnp.bfloat16, jnp.float32
        dma = pltpu.SemaphoreType.DMA
        packet = (n, per, CAP, rows, width)
        grouped = (
            [pltpu.VMEM(packet, bf16)] * (2 * groups)
            + [pltpu.VMEM((n, 1, stat_lanes), f32)] * groups
        )
        weight = out_weight.reshape(nh, groups, per * width, cols)
        return pl.pallas_call(
            functools.partial(kernel, (n, nh, heads, tiles, rows, width, groups)),
            out_shape=jax.ShapeDtypeStruct((tokens, cols), bf16),
            in_specs=[pl.BlockSpec(memory_space=pltpu.VMEM)]
            + [pl.BlockSpec(memory_space=pl.ANY)] * 4,
            out_specs=pl.BlockSpec(memory_space=pltpu.VMEM),
            scratch_shapes=[
                pltpu.VMEM((tiles, rows, heads * width), bf16),
                pltpu.VMEM((tokens, heads * width), bf16),
                pltpu.VMEM((tokens, heads * width), bf16),
                pltpu.VMEM(weight.shape, bf16),
                pltpu.VMEM((groups,) + packet, bf16),
                pltpu.VMEM((groups,) + packet, bf16),
                pltpu.VMEM((groups, n, 1, stat_lanes), f32),
                pltpu.VMEM((heads, tiles, rows, width), f32),
                pltpu.VMEM((heads, tiles, rows, width), f32),
                pltpu.VMEM((nh, groups, tokens, per * width), bf16),
                pltpu.VMEM((tokens, cols), f32),
                pltpu.VMEM(table, jnp.int32),
                pltpu.SMEM(table, jnp.int32),
                dma((5,)),
                dma((groups, n)),
                dma((groups, n)),
                dma((groups, n)),
                dma((groups, n)),
                dma((groups, n)),
                dma((groups, n)),
                dma((nh, groups)),
                dma((nh, groups)),
            ]
            + grouped,
            compiler_params=pltpu.CompilerParams(
                collective_id=0, has_side_effects=True, vmem_limit_bytes=56 * 1024 * 1024
            ),
        )(
            jnp.transpose(selected, (2, 0, 1)),
            queries.reshape(tiles, rows, heads * width),
            keys,
            values,
            weight,
        )

    return jax.shard_map(
        local,
        mesh=mesh,
        in_specs=(
            P("ctx", "head"),
            P("ctx", "head"),
            P("ctx", "head"),
            P("head", "ctx", None),
            P(None, "head"),
        ),
        out_specs=P("ctx", "head"),
        check_vma=False,
    )
```

```python
import functools

import jax
import jax.numpy as jnp
from jax import lax
from jax.experimental import pallas as pl
from jax.experimental.pallas import tpu as pltpu
from jax.sharding import PartitionSpec as P

CAP = 2
AHEAD = 4
LAG = 2
TEAM = 4
MESH = pl.DeviceIdType.MESH
LOG2E = 1.4426950408889634
NT = (((1,), (1,)), ((), ()))


def softmax_block(query, key, value, scale, mask):
    scores = lax.dot_general(query, key, NT, preferred_element_type=jnp.float32)
    if mask is not None:
        scores = jnp.where(mask, scores, jnp.float32(-1e30))
    top = jnp.max(scores, axis=-1, keepdims=True)
    prob = jnp.exp2((scores - top) * (scale * LOG2E))
    total = jnp.sum(prob, axis=-1, keepdims=True)
    part = jnp.dot(prob.astype(jnp.bfloat16), value, preferred_element_type=jnp.float32)
    return part * (1.0 / total), top, total


def fill_tables(n, tiles, sel, tblv):
    each, heads, _ = sel.shape
    entries = (each - 1) * tiles
    lane = lax.broadcasted_iota(jnp.int32, (heads, entries), 1)
    picks = jnp.zeros((heads, entries), jnp.int32)
    tile_of = lane
    column = []
    for r in range(1, each):
        chosen = sel[r]
        tile_of = jnp.where(lane >= (r - 1) * tiles, lane - (r - 1) * tiles, tile_of)
        for t in range(tiles):
            column.append(chosen[:, t : t + 1])
            picks = jnp.where(lane == (r - 1) * tiles + t, column[-1], picks)
    rank = jnp.zeros((heads, entries), jnp.int32)
    for j in range(entries):
        rank += jnp.where((picks == column[j]) & (lane > j), 1, 0)
    slot = jnp.minimum(rank, CAP - 1)
    lanes = tblv.shape[2]
    wide = lax.broadcasted_iota(jnp.int32, (heads, lanes), 1)
    found = jnp.zeros((heads, lanes), jnp.int32)
    for a in range(n):
        for s in range(CAP):
            hit = (picks == a) & (slot == s)
            tile = jnp.max(jnp.where(hit, tile_of, 0), axis=1, keepdims=True)
            found = jnp.where(wide == a * CAP + s, tile, found)
    tblv[0] = found
    tblv[1] = jnp.zeros((heads, lanes), jnp.int32)
    tblv[2] = jnp.zeros((heads, lanes), jnp.int32)
    tblv[1, :, :entries] = picks
    tblv[2, :, :entries] = slot


def kernel(
    dims,
    sel,
    q_hbm,
    k_hbm,
    v_hbm,
    w_hbm,
    out_ref,
    q,
    k,
    v,
    w,
    qsend,
    osend,
    ssend,
    own,
    own_lse,
    att,
    acc,
    tblv,
    tbl,
    load_sem,
    qs_sem,
    qr_sem,
    os_sem,
    or_sem,
    ss_sem,
    sr_sem,
    as_sem,
    ar_sem,
    *grouped,
):
    n, nh, heads, tiles, rows, width, groups = dims
    per = heads // groups
    tokens = tiles * rows
    scale = width ** (-0.5)
    qrecv, orecv, srecv = (grouped[i * groups : (i + 1) * groups] for i in range(3))
    me = lax.axis_index("ctx")
    hd = lax.axis_index("head")

    loads = [
        pltpu.make_async_copy(src, dst, load_sem.at[i])
        for i, (src, dst) in enumerate(((q_hbm, q), (k_hbm, k), (v_hbm, v), (w_hbm, w)))
    ]
    for copy in loads:
        copy.start()

    barrier = pltpu.get_barrier_semaphore()

    def greet(d, _):
        pl.semaphore_signal(
            barrier, inc=1, device_id={"ctx": lax.rem(me + d, n)}, device_id_type=MESH
        )
        return 0

    lax.fori_loop(1, n, greet, 0)
    for j in range(1, nh):
        pl.semaphore_signal(
            barrier, inc=1, device_id={"head": lax.rem(hd + j, nh)}, device_id_type=MESH
        )

    level, place = me // TEAM, lax.rem(me, TEAM)
    levels = n // TEAM

    def distance(i):
        half = (i + 1) // 2
        return levels // 2 + jnp.where(i % 2 == 0, half, -half)

    def member(at_level, j):
        return at_level * TEAM + lax.rem(place + j, TEAM)

    def q_copy(g, there, here):
        return pltpu.make_async_remote_copy(
            src_ref=qsend.at[g, there],
            dst_ref=qrecv[g].at[here],
            send_sem=qs_sem.at[g, there],
            recv_sem=qr_sem.at[g, here],
            device_id={"ctx": there},
            device_id_type=MESH,
        )

    def o_copy(g, there, here):
        return pltpu.make_async_remote_copy(
            src_ref=osend.at[g, there],
            dst_ref=orecv[g].at[here],
            send_sem=os_sem.at[g, there],
            recv_sem=or_sem.at[g, here],
            device_id={"ctx": there},
            device_id_type=MESH,
        )

    def s_copy(g, there, here):
        return pltpu.make_async_remote_copy(
            src_ref=ssend.at[g, there],
            dst_ref=srecv[g].at[here],
            send_sem=ss_sem.at[g, there],
            recv_sem=sr_sem.at[g, here],
            device_id={"ctx": there},
            device_id_type=MESH,
        )

    def a_copy(g, there, here):
        return pltpu.make_async_remote_copy(
            src_ref=att.at[here, g],
            dst_ref=att.at[here, g],
            send_sem=as_sem.at[there, g],
            recv_sem=ar_sem.at[here, g],
            device_id={"head": there},
            device_id_type=MESH,
        )

    fill_tables(n, tiles, sel, tblv)
    to_scalars = pltpu.make_async_copy(tblv, tbl, load_sem.at[4])
    to_scalars.start()
    loads[0].wait()
    to_scalars.wait()
    pl.semaphore_wait(barrier, n - 1 + nh - 1)

    def send_group(g):
        def send_queries(i, _):
            there = member(level - distance(i // TEAM), lax.rem(i, TEAM))

            @pl.when((there >= 0) & (there < me))
            def _():
                for hh in range(per):
                    h = g * per + hh
                    for s in range(CAP):
                        tile = tbl[0, h, there * CAP + s]
                        qsend[g, there, hh, s] = q[tile, :, h * width : (h + 1) * width]
                q_copy(g, there, me).start()

            return 0

        lax.fori_loop(0, n, send_queries, 0)

    for g in range(min(AHEAD, groups)):
        send_group(g)
    loads[1].wait()
    loads[2].wait()
    causal = lax.broadcasted_iota(jnp.int32, (tokens, tokens), 0) >= lax.broadcasted_iota(
        jnp.int32, (tokens, tokens), 1
    )
    def own_group(g):
        for h in range(g * per, (g + 1) * per):
            cols = slice(h * width, (h + 1) * width)
            query = q[:, :, cols].reshape(tokens, width)
            part, top, total = softmax_block(query, k[:, cols], v[:, cols], scale, causal)
            lse = top * scale + jnp.log(total)
            own[h] = part.reshape(tiles, rows, width)
            own_lse[h] = jnp.broadcast_to(lse, (tokens, width)).reshape(tiles, rows, width)

    short = CAP * rows
    stat_lanes = ssend.shape[3]
    lane = lax.broadcasted_iota(jnp.int32, (TEAM, short, 128), 2)
    lane = lane - lax.broadcasted_iota(jnp.int32, (TEAM, short, 128), 1)

    def as_row(hit, column):
        column = jnp.broadcast_to(column, (TEAM * short, 128)).reshape(TEAM, short, 128)
        return jnp.sum(jnp.where(hit, column, 0.0), axis=1, keepdims=True)

    def answer_group(g):
        orecv[g][me] = jnp.zeros((per, CAP, rows, width), jnp.bfloat16)
        srecv[g][me] = jnp.full((1, stat_lanes), -1e30, jnp.float32)

        def answer(i, _):
            their = level + distance(i)

            @pl.when(their < levels)
            def _():
                for j in range(TEAM):
                    there = member(their, j)

                    @pl.when(there > me)
                    def _():
                        q_copy(g, me, there).wait_recv()

                team = pl.ds(pl.multiple_of(their * TEAM, TEAM), TEAM)
                both = 128 // short
                for first in range(0, per, both):
                    tops = jnp.zeros((TEAM, 1, 128), jnp.float32)
                    totals = jnp.zeros((TEAM, 1, 128), jnp.float32)
                    for hh in range(first, min(first + both, per)):
                        h = g * per + hh
                        cols = slice(h * width, (h + 1) * width)
                        query = qrecv[g][team, hh].reshape(TEAM * short, width)
                        part, top, total = softmax_block(query, k[:, cols], v[:, cols], scale, None)
                        part = part.astype(jnp.bfloat16).reshape(TEAM, CAP, rows, width)
                        osend[g, team, hh] = part
                        hit = lane == (hh - first) * short
                        tops += as_row(hit, top)
                        totals += as_row(hit, total)
                    ssend[g, team, :, first * short : first * short + 128] = tops * scale + jnp.log(
                        totals
                    )
                for j in range(TEAM):
                    there = member(their, j)

                    @pl.when(there > me)
                    def _():
                        o_copy(g, there, me).start()
                        s_copy(g, there, me).start()

            return 0

        lax.fori_loop(0, levels, answer, 0)

    part_cols = min(256, out_ref.shape[1])

    def project(p, last):
        def body(c, _):
            at = pl.ds(pl.multiple_of(c * part_cols, part_cols), part_cols)
            term = 0.0 if p is hd else acc[:, at]
            for g in range(groups):
                term += jnp.dot(att[p, g], w[p, g, :, at], preferred_element_type=jnp.float32)
            if last:
                out_ref[:, at] = term.astype(out_ref.dtype)
            else:
                acc[:, at] = term
            return 0

        lax.fori_loop(0, out_ref.shape[1] // part_cols, body, 0)

    lane_tile = lax.broadcasted_iota(jnp.int32, (rows, 128), 1)
    lane_tile = lane_tile - lax.broadcasted_iota(jnp.int32, (rows, 128), 0)

    def collect_group(g):
        def collect(i, _):
            there = member(level - distance(i // TEAM), lax.rem(i, TEAM))

            @pl.when((there >= 0) & (there < me))
            def _():
                s_copy(g, me, there).wait_recv()
                o_copy(g, me, there).wait_recv()

            return 0

        lax.fori_loop(0, n, collect, 0)

        def picked_lse(block, slot, hh):
            at = hh * short // 128 * 128
            hit = lane_tile == hh * short - at + slot * rows
            row = srecv[g][block][:, at : at + 128]
            return jnp.sum(jnp.where(hit, row, 0.0), axis=1, keepdims=True)

        for hh in range(per):
            h = g * per + hh

            def gather(r):
                blocks = [tbl[1, h, (r - 1) * tiles + t] for t in range(tiles)]
                slots = [tbl[2, h, (r - 1) * tiles + t] for t in range(tiles)]
                outs = [orecv[g][a, hh, s] for a, s in zip(blocks, slots)]
                lses = [picked_lse(a, s, hh) for a, s in zip(blocks, slots)]
                return jnp.concatenate(outs, 0).astype(jnp.float32), jnp.concatenate(lses, 0)

            (o1, l1), (o2, l2) = gather(1), gather(2)
            l0 = own_lse[h].reshape(tokens, width)
            top = jnp.maximum(l0, jnp.maximum(l1, l2))
            w0, w1, w2 = jnp.exp(l0 - top), jnp.exp(l1 - top), jnp.exp(l2 - top)
            mixed = w0 * own[h].reshape(tokens, width) + w1 * o1 + w2 * o2
            mixed = mixed / (w0 + w1 + w2)
            att[hd, g, :, hh * width : (hh + 1) * width] = mixed.astype(jnp.bfloat16)
        for j in range(1, nh):
            a_copy(g, lax.rem(hd + j, nh), hd).start()

    own_group(0)
    for g in range(groups):
        answer_group(g)
        if g + AHEAD < groups:
            send_group(g + AHEAD)
        if g + 1 < groups:
            own_group(g + 1)
        if g >= LAG:
            collect_group(g - LAG)
    for g in range(max(groups - LAG, 0), groups):
        collect_group(g)
    loads[3].wait()
    project(hd, nh == 1)
    for g in range(groups):

        def drain(d, _, g=g):
            @pl.when(me - d >= 0)
            def _():
                q_copy(g, me - d, me).wait_send()

            @pl.when(me + d < n)
            def _():
                o_copy(g, me + d, me).wait_send()
                s_copy(g, me + d, me).wait_send()

            return 0

        lax.fori_loop(1, n, drain, 0)

    for j in range(1, nh):
        peer = lax.rem(hd + j, nh)
        for g in range(groups):
            a_copy(g, hd, peer).wait_recv()
        project(peer, j == nh - 1)

    for g in range(groups):
        for j in range(1, nh):
            a_copy(g, lax.rem(hd + j, nh), hd).wait_send()


def solution(mesh):
    n, nh = mesh.shape["ctx"], mesh.shape["head"]

    def local(queries, keys, values, selected, out_weight):
        heads, tiles = selected.shape[:2]
        tokens, cols = queries.shape[0], out_weight.shape[1]
        width = queries.shape[1] // heads
        rows = tokens // tiles
        per = 1
        groups = heads // per
        stat_lanes = -(-per * CAP * rows // 128) * 128
        table = (3, heads, -(-max(n * CAP, tiles * 3) // 128) * 128)
        bf16, f32 = jnp.bfloat16, jnp.float32
        dma = pltpu.SemaphoreType.DMA
        packet = (n, per, CAP, rows, width)
        grouped = (
            [pltpu.VMEM(packet, bf16)] * (2 * groups)
            + [pltpu.VMEM((n, 1, stat_lanes), f32)] * groups
        )
        weight = out_weight.reshape(nh, groups, per * width, cols)
        return pl.pallas_call(
            functools.partial(kernel, (n, nh, heads, tiles, rows, width, groups)),
            out_shape=jax.ShapeDtypeStruct((tokens, cols), bf16),
            in_specs=[pl.BlockSpec(memory_space=pltpu.VMEM)]
            + [pl.BlockSpec(memory_space=pl.ANY)] * 4,
            out_specs=pl.BlockSpec(memory_space=pltpu.VMEM),
            scratch_shapes=[
                pltpu.VMEM((tiles, rows, heads * width), bf16),
                pltpu.VMEM((tokens, heads * width), bf16),
                pltpu.VMEM((tokens, heads * width), bf16),
                pltpu.VMEM(weight.shape, bf16),
                pltpu.VMEM((groups,) + packet, bf16),
                pltpu.VMEM((groups,) + packet, bf16),
                pltpu.VMEM((groups, n, 1, stat_lanes), f32),
                pltpu.VMEM((heads, tiles, rows, width), f32),
                pltpu.VMEM((heads, tiles, rows, width), f32),
                pltpu.VMEM((nh, groups, tokens, per * width), bf16),
                pltpu.VMEM((tokens, cols), f32),
                pltpu.VMEM(table, jnp.int32),
                pltpu.SMEM(table, jnp.int32),
                dma((5,)),
                dma((groups, n)),
                dma((groups, n)),
                dma((groups, n)),
                dma((groups, n)),
                dma((groups, n)),
                dma((groups, n)),
                dma((nh, groups)),
                dma((nh, groups)),
            ]
            + grouped,
            compiler_params=pltpu.CompilerParams(
                collective_id=0, has_side_effects=True, vmem_limit_bytes=56 * 1024 * 1024
            ),
        )(
            jnp.transpose(selected, (2, 0, 1)),
            queries.reshape(tiles, rows, heads * width),
            keys,
            values,
            weight,
        )

    return jax.shard_map(
        local,
        mesh=mesh,
        in_specs=(
            P("ctx", "head"),
            P("ctx", "head"),
            P("ctx", "head"),
            P("head", "ctx", None),
            P(None, "head"),
        ),
        out_specs=P("ctx", "head"),
        check_vma=False,
    )
```

```python
import functools

import jax
import jax.numpy as jnp
from jax import lax
from jax.experimental import pallas as pl
from jax.experimental.pallas import tpu as pltpu
from jax.sharding import PartitionSpec as P

CAP = 2
LAG = 1
TEAM = 4
MESH = pl.DeviceIdType.MESH
LOG2E = 1.4426950408889634
NT = (((1,), (1,)), ((), ()))


def softmax_block(query, key, value, scale, mask):
    scores = lax.dot_general(query, key, NT, preferred_element_type=jnp.float32)
    if mask is not None:
        scores = jnp.where(mask, scores, jnp.float32(-1e30))
    top = jnp.max(scores, axis=-1, keepdims=True)
    prob = jnp.exp2((scores - top) * (scale * LOG2E))
    total = jnp.sum(prob, axis=-1, keepdims=True)
    part = jnp.dot(prob.astype(jnp.bfloat16), value, preferred_element_type=jnp.float32)
    return part * (1.0 / total), top, total


def fill_tables(n, tiles, sel, tblv):
    each, heads, _ = sel.shape
    entries = (each - 1) * tiles
    lane = lax.broadcasted_iota(jnp.int32, (heads, entries), 1)
    picks = jnp.zeros((heads, entries), jnp.int32)
    tile_of = lane
    column = []
    for r in range(1, each):
        chosen = sel[r]
        tile_of = jnp.where(lane >= (r - 1) * tiles, lane - (r - 1) * tiles, tile_of)
        for t in range(tiles):
            column.append(chosen[:, t : t + 1])
            picks = jnp.where(lane == (r - 1) * tiles + t, column[-1], picks)
    rank = jnp.zeros((heads, entries), jnp.int32)
    for j in range(entries):
        rank += jnp.where((picks == column[j]) & (lane > j), 1, 0)
    slot = jnp.minimum(rank, CAP - 1)
    lanes = tblv.shape[2]
    wide = lax.broadcasted_iota(jnp.int32, (heads, lanes), 1)
    found = jnp.zeros((heads, lanes), jnp.int32)
    for a in range(n):
        for s in range(CAP):
            hit = (picks == a) & (slot == s)
            tile = jnp.max(jnp.where(hit, tile_of, 0), axis=1, keepdims=True)
            found = jnp.where(wide == a * CAP + s, tile, found)
    tblv[0] = found
    tblv[1] = jnp.zeros((heads, lanes), jnp.int32)
    tblv[2] = jnp.zeros((heads, lanes), jnp.int32)
    tblv[1, :, :entries] = picks
    tblv[2, :, :entries] = slot


def kernel(
    dims,
    sel,
    q_hbm,
    k_hbm,
    v_hbm,
    w_hbm,
    out_ref,
    q,
    k,
    v,
    w,
    qsend,
    osend,
    ssend,
    own,
    own_lse,
    att,
    acc,
    tblv,
    tbl,
    load_sem,
    qs_sem,
    qr_sem,
    os_sem,
    or_sem,
    ss_sem,
    sr_sem,
    as_sem,
    ar_sem,
    *grouped,
):
    n, nh, heads, tiles, rows, width, groups = dims
    per = heads // groups
    tokens = tiles * rows
    scale = width ** (-0.5)
    qrecv, orecv, srecv = (grouped[i * groups : (i + 1) * groups] for i in range(3))
    me = lax.axis_index("ctx")
    hd = lax.axis_index("head")

    loads = [
        pltpu.make_async_copy(src, dst, load_sem.at[i])
        for i, (src, dst) in enumerate(((q_hbm, q), (k_hbm, k), (v_hbm, v), (w_hbm, w)))
    ]
    for copy in loads:
        copy.start()

    barrier = pltpu.get_barrier_semaphore()

    def greet(d, _):
        pl.semaphore_signal(
            barrier, inc=1, device_id={"ctx": lax.rem(me + d, n)}, device_id_type=MESH
        )
        return 0

    lax.fori_loop(1, n, greet, 0)
    for j in range(1, nh):
        pl.semaphore_signal(
            barrier, inc=1, device_id={"head": lax.rem(hd + j, nh)}, device_id_type=MESH
        )

    level, place = me // TEAM, lax.rem(me, TEAM)
    levels = n // TEAM

    def distance(i):
        half = (i + 1) // 2
        return levels // 2 + jnp.where(i % 2 == 0, half, -half)

    def member(at_level, j):
        return at_level * TEAM + lax.rem(place + j, TEAM)

    def q_copy(g, there, here):
        return pltpu.make_async_remote_copy(
            src_ref=qsend.at[g, there],
            dst_ref=qrecv[g].at[here],
            send_sem=qs_sem.at[g, there],
            recv_sem=qr_sem.at[g, here],
            device_id={"ctx": there},
            device_id_type=MESH,
        )

    def o_copy(g, there, here):
        return pltpu.make_async_remote_copy(
            src_ref=osend.at[g, there],
            dst_ref=orecv[g].at[here],
            send_sem=os_sem.at[g, there],
            recv_sem=or_sem.at[g, here],
            device_id={"ctx": there},
            device_id_type=MESH,
        )

    def s_copy(g, there, here):
        return pltpu.make_async_remote_copy(
            src_ref=ssend.at[g, there],
            dst_ref=srecv[g].at[here],
            send_sem=ss_sem.at[g, there],
            recv_sem=sr_sem.at[g, here],
            device_id={"ctx": there},
            device_id_type=MESH,
        )

    def a_copy(g, there, here):
        return pltpu.make_async_remote_copy(
            src_ref=att.at[here, g],
            dst_ref=att.at[here, g],
            send_sem=as_sem.at[there, g],
            recv_sem=ar_sem.at[here, g],
            device_id={"head": there},
            device_id_type=MESH,
        )

    fill_tables(n, tiles, sel, tblv)
    to_scalars = pltpu.make_async_copy(tblv, tbl, load_sem.at[4])
    to_scalars.start()
    loads[0].wait()
    to_scalars.wait()
    pl.semaphore_wait(barrier, n - 1 + nh - 1)

    def send_group(g):
        def send_queries(i, _):
            there = member(level - distance(i // TEAM), lax.rem(i, TEAM))

            @pl.when((there >= 0) & (there < me))
            def _():
                for hh in range(per):
                    h = g * per + hh
                    for s in range(CAP):
                        tile = tbl[0, h, there * CAP + s]
                        qsend[g, there, hh, s] = q[tile, :, h * width : (h + 1) * width]
                q_copy(g, there, me).start()

            return 0

        lax.fori_loop(0, n, send_queries, 0)

    for g in range(groups):
        send_group(g)
    loads[1].wait()
    loads[2].wait()
    causal = lax.broadcasted_iota(jnp.int32, (tokens, tokens), 0) >= lax.broadcasted_iota(
        jnp.int32, (tokens, tokens), 1
    )
    def own_group(g):
        for h in range(g * per, (g + 1) * per):
            cols = slice(h * width, (h + 1) * width)
            query = q[:, :, cols].reshape(tokens, width)
            part, top, total = softmax_block(query, k[:, cols], v[:, cols], scale, causal)
            lse = top * scale + jnp.log(total)
            own[h] = part.reshape(tiles, rows, width)
            own_lse[h] = jnp.broadcast_to(lse, (tokens, width)).reshape(tiles, rows, width)

    short = CAP * rows
    stat_lanes = ssend.shape[3]
    lane = lax.broadcasted_iota(jnp.int32, (TEAM, short, 128), 2)
    lane = lane - lax.broadcasted_iota(jnp.int32, (TEAM, short, 128), 1)

    def as_row(hit, column):
        column = jnp.broadcast_to(column, (TEAM * short, 128)).reshape(TEAM, short, 128)
        return jnp.sum(jnp.where(hit, column, 0.0), axis=1, keepdims=True)

    def clear_group(g):
        orecv[g][me] = jnp.zeros((per, CAP, rows, width), jnp.bfloat16)
        srecv[g][me] = jnp.full((1, stat_lanes), -1e30, jnp.float32)

    def answer_team(g, their, wanted):
        def answer():
            @pl.when(wanted)
            def _():
                for j in range(TEAM):
                    there = member(their, j)

                    @pl.when(there > me)
                    def _():
                        q_copy(g, me, there).wait_recv()

                team = pl.ds(pl.multiple_of(their * TEAM, TEAM), TEAM)
                both = 128 // short
                for first in range(0, per, both):
                    tops = jnp.zeros((TEAM, 1, 128), jnp.float32)
                    totals = jnp.zeros((TEAM, 1, 128), jnp.float32)
                    for hh in range(first, min(first + both, per)):
                        h = g * per + hh
                        cols = slice(h * width, (h + 1) * width)
                        query = qrecv[g][team, hh].reshape(TEAM * short, width)
                        part, top, total = softmax_block(query, k[:, cols], v[:, cols], scale, None)
                        part = part.astype(jnp.bfloat16).reshape(TEAM, CAP, rows, width)
                        osend[g, team, hh] = part
                        hit = lane == (hh - first) * short
                        tops += as_row(hit, top)
                        totals += as_row(hit, total)
                    ssend[g, team, :, first * short : first * short + 128] = tops * scale + jnp.log(
                        totals
                    )
                for j in range(TEAM):
                    there = member(their, j)

                    @pl.when(there > me)
                    def _():
                        o_copy(g, there, me).start()
                        s_copy(g, there, me).start()

        answer()

    part_cols = min(256, out_ref.shape[1])

    def project(p, last):
        def body(c, _):
            at = pl.ds(pl.multiple_of(c * part_cols, part_cols), part_cols)
            term = 0.0 if p is hd else acc[:, at]
            for g in range(groups):
                term += jnp.dot(att[p, g], w[p, g, :, at], preferred_element_type=jnp.float32)
            if last:
                out_ref[:, at] = term.astype(out_ref.dtype)
            else:
                acc[:, at] = term
            return 0

        lax.fori_loop(0, out_ref.shape[1] // part_cols, body, 0)

    lane_tile = lax.broadcasted_iota(jnp.int32, (rows, 128), 1)
    lane_tile = lane_tile - lax.broadcasted_iota(jnp.int32, (rows, 128), 0)

    def collect_group(g):
        def collect(i, _):
            there = member(level - distance(i // TEAM), lax.rem(i, TEAM))

            @pl.when((there >= 0) & (there < me))
            def _():
                s_copy(g, me, there).wait_recv()
                o_copy(g, me, there).wait_recv()

            return 0

        lax.fori_loop(0, n, collect, 0)

        def picked_lse(block, slot, hh):
            at = hh * short // 128 * 128
            hit = lane_tile == hh * short - at + slot * rows
            row = srecv[g][block][:, at : at + 128]
            return jnp.sum(jnp.where(hit, row, 0.0), axis=1, keepdims=True)

        for hh in range(per):
            h = g * per + hh

            def gather(r):
                blocks = [tbl[1, h, (r - 1) * tiles + t] for t in range(tiles)]
                slots = [tbl[2, h, (r - 1) * tiles + t] for t in range(tiles)]
                outs = [orecv[g][a, hh, s] for a, s in zip(blocks, slots)]
                lses = [picked_lse(a, s, hh) for a, s in zip(blocks, slots)]
                return jnp.concatenate(outs, 0).astype(jnp.float32), jnp.concatenate(lses, 0)

            (o1, l1), (o2, l2) = gather(1), gather(2)
            l0 = own_lse[h].reshape(tokens, width)
            top = jnp.maximum(l0, jnp.maximum(l1, l2))
            w0, w1, w2 = jnp.exp(l0 - top), jnp.exp(l1 - top), jnp.exp(l2 - top)
            mixed = w0 * own[h].reshape(tokens, width) + w1 * o1 + w2 * o2
            mixed = mixed / (w0 + w1 + w2)
            att[hd, g, :, hh * width : (hh + 1) * width] = mixed.astype(jnp.bfloat16)
        for j in range(1, nh):
            a_copy(g, lax.rem(hd + j, nh), hd).start()

    top_level = levels - 1
    for g in range(groups):
        clear_group(g)

        def answer_between(i, _, g=g):
            their = level + distance(i)
            answer_team(g, their, (their > level) & (their < top_level))
            return 0

        lax.fori_loop(0, levels, answer_between, 0)
        own_group(g)
    for g in range(groups):

        def answer_rest(i, _, g=g):
            their = jnp.where(i == 0, top_level, level)
            answer_team(g, their, (i == 1) | (their > level))
            return 0

        lax.fori_loop(0, 2, answer_rest, 0)
        if g >= LAG:
            collect_group(g - LAG)
    for g in range(max(groups - LAG, 0), groups):
        collect_group(g)
    loads[3].wait()
    project(hd, nh == 1)
    for g in range(groups):

        def drain(d, _, g=g):
            @pl.when(me - d >= 0)
            def _():
                q_copy(g, me - d, me).wait_send()

            @pl.when(me + d < n)
            def _():
                o_copy(g, me + d, me).wait_send()
                s_copy(g, me + d, me).wait_send()

            return 0

        lax.fori_loop(1, n, drain, 0)

    for j in range(1, nh):
        peer = lax.rem(hd + j, nh)
        for g in range(groups):
            a_copy(g, hd, peer).wait_recv()
        project(peer, j == nh - 1)

    for g in range(groups):
        for j in range(1, nh):
            a_copy(g, lax.rem(hd + j, nh), hd).wait_send()


def solution(mesh):
    n, nh = mesh.shape["ctx"], mesh.shape["head"]

    def local(queries, keys, values, selected, out_weight):
        heads, tiles = selected.shape[:2]
        tokens, cols = queries.shape[0], out_weight.shape[1]
        width = queries.shape[1] // heads
        rows = tokens // tiles
        per = 2 if heads % 4 == 0 else 1
        groups = heads // per
        stat_lanes = -(-per * CAP * rows // 128) * 128
        table = (3, heads, -(-max(n * CAP, tiles * 3) // 128) * 128)
        bf16, f32 = jnp.bfloat16, jnp.float32
        dma = pltpu.SemaphoreType.DMA
        packet = (n, per, CAP, rows, width)
        grouped = (
            [pltpu.VMEM(packet, bf16)] * (2 * groups)
            + [pltpu.VMEM((n, 1, stat_lanes), f32)] * groups
        )
        weight = out_weight.reshape(nh, groups, per * width, cols)
        return pl.pallas_call(
            functools.partial(kernel, (n, nh, heads, tiles, rows, width, groups)),
            out_shape=jax.ShapeDtypeStruct((tokens, cols), bf16),
            in_specs=[pl.BlockSpec(memory_space=pltpu.VMEM)]
            + [pl.BlockSpec(memory_space=pl.ANY)] * 4,
            out_specs=pl.BlockSpec(memory_space=pltpu.VMEM),
            scratch_shapes=[
                pltpu.VMEM((tiles, rows, heads * width), bf16),
                pltpu.VMEM((tokens, heads * width), bf16),
                pltpu.VMEM((tokens, heads * width), bf16),
                pltpu.VMEM(weight.shape, bf16),
                pltpu.VMEM((groups,) + packet, bf16),
                pltpu.VMEM((groups,) + packet, bf16),
                pltpu.VMEM((groups, n, 1, stat_lanes), f32),
                pltpu.VMEM((heads, tiles, rows, width), f32),
                pltpu.VMEM((heads, tiles, rows, width), f32),
                pltpu.VMEM((nh, groups, tokens, per * width), bf16),
                pltpu.VMEM((tokens, cols), f32),
                pltpu.VMEM(table, jnp.int32),
                pltpu.SMEM(table, jnp.int32),
                dma((5,)),
                dma((groups, n)),
                dma((groups, n)),
                dma((groups, n)),
                dma((groups, n)),
                dma((groups, n)),
                dma((groups, n)),
                dma((nh, groups)),
                dma((nh, groups)),
            ]
            + grouped,
            compiler_params=pltpu.CompilerParams(
                collective_id=0, has_side_effects=True, vmem_limit_bytes=56 * 1024 * 1024
            ),
        )(
            jnp.transpose(selected, (2, 0, 1)),
            queries.reshape(tiles, rows, heads * width),
            keys,
            values,
            weight,
        )

    return jax.shard_map(
        local,
        mesh=mesh,
        in_specs=(
            P("ctx", "head"),
            P("ctx", "head"),
            P("ctx", "head"),
            P("head", "ctx", None),
            P(None, "head"),
        ),
        out_specs=P("ctx", "head"),
        check_vma=False,
    )
```

```python
import functools

import jax
import jax.numpy as jnp
from jax import lax
from jax.experimental import pallas as pl
from jax.experimental.pallas import tpu as pltpu
from jax.sharding import PartitionSpec as P

CAP = 2
AHEAD = 4
LAG = 2
TEAM = 4
MESH = pl.DeviceIdType.MESH
LOG2E = 1.4426950408889634
NT = (((1,), (1,)), ((), ()))


def softmax_block(query, key, value, scale, mask):
    scores = lax.dot_general(query, key, NT, preferred_element_type=jnp.float32)
    if mask is not None:
        scores = jnp.where(mask, scores, jnp.float32(-1e30))
    top = jnp.max(scores, axis=-1, keepdims=True)
    prob = jnp.exp2((scores - top) * (scale * LOG2E))
    total = jnp.sum(prob, axis=-1, keepdims=True)
    part = jnp.dot(prob.astype(jnp.bfloat16), value, preferred_element_type=jnp.float32)
    return part * (1.0 / total), top, total


def fill_tables(n, tiles, sel, tblv):
    each, heads, _ = sel.shape
    entries = (each - 1) * tiles
    lane = lax.broadcasted_iota(jnp.int32, (heads, entries), 1)
    picks = jnp.zeros((heads, entries), jnp.int32)
    tile_of = lane
    column = []
    for r in range(1, each):
        chosen = sel[r]
        tile_of = jnp.where(lane >= (r - 1) * tiles, lane - (r - 1) * tiles, tile_of)
        for t in range(tiles):
            column.append(chosen[:, t : t + 1])
            picks = jnp.where(lane == (r - 1) * tiles + t, column[-1], picks)
    rank = jnp.zeros((heads, entries), jnp.int32)
    for j in range(entries):
        rank += jnp.where((picks == column[j]) & (lane > j), 1, 0)
    slot = jnp.minimum(rank, CAP - 1)
    lanes = tblv.shape[2]
    wide = lax.broadcasted_iota(jnp.int32, (heads, lanes), 1)
    found = jnp.zeros((heads, lanes), jnp.int32)
    for a in range(n):
        for s in range(CAP):
            hit = (picks == a) & (slot == s)
            tile = jnp.max(jnp.where(hit, tile_of, 0), axis=1, keepdims=True)
            found = jnp.where(wide == a * CAP + s, tile, found)
    tblv[0] = found
    tblv[1] = jnp.zeros((heads, lanes), jnp.int32)
    tblv[2] = jnp.zeros((heads, lanes), jnp.int32)
    tblv[1, :, :entries] = picks
    tblv[2, :, :entries] = slot


def kernel(
    dims,
    sel,
    q_hbm,
    k_hbm,
    v_hbm,
    w_hbm,
    out_ref,
    q,
    k,
    v,
    w,
    qsend,
    osend,
    ssend,
    own,
    own_lse,
    att,
    acc,
    tblv,
    tbl,
    load_sem,
    qs_sem,
    qr_sem,
    os_sem,
    or_sem,
    ss_sem,
    sr_sem,
    as_sem,
    ar_sem,
    *grouped,
):
    n, nh, heads, tiles, rows, width, groups = dims
    per = heads // groups
    tokens = tiles * rows
    scale = width ** (-0.5)
    qrecv, orecv, srecv = (grouped[i * groups : (i + 1) * groups] for i in range(3))
    me = lax.axis_index("ctx")
    hd = lax.axis_index("head")

    loads = [
        pltpu.make_async_copy(src, dst, load_sem.at[i])
        for i, (src, dst) in enumerate(((q_hbm, q), (k_hbm, k), (v_hbm, v), (w_hbm, w)))
    ]
    for copy in loads:
        copy.start()

    barrier = pltpu.get_barrier_semaphore()

    def greet(d, _):
        pl.semaphore_signal(
            barrier, inc=1, device_id={"ctx": lax.rem(me + d, n)}, device_id_type=MESH
        )
        return 0

    lax.fori_loop(1, n, greet, 0)
    for j in range(1, nh):
        pl.semaphore_signal(
            barrier, inc=1, device_id={"head": lax.rem(hd + j, nh)}, device_id_type=MESH
        )

    level, place = me // TEAM, lax.rem(me, TEAM)
    levels = n // TEAM

    def distance(i):
        half = (i + 1) // 2
        return levels // 2 + jnp.where(i % 2 == 0, -half, half)

    def member(at_level, j):
        return at_level * TEAM + lax.rem(place + j, TEAM)

    def q_copy(g, there, here):
        return pltpu.make_async_remote_copy(
            src_ref=qsend.at[g, there],
            dst_ref=qrecv[g].at[here],
            send_sem=qs_sem.at[g, there],
            recv_sem=qr_sem.at[g, here],
            device_id={"ctx": there},
            device_id_type=MESH,
        )

    def o_copy(g, there, here):
        return pltpu.make_async_remote_copy(
            src_ref=osend.at[g, there],
            dst_ref=orecv[g].at[here],
            send_sem=os_sem.at[g, there],
            recv_sem=or_sem.at[g, here],
            device_id={"ctx": there},
            device_id_type=MESH,
        )

    def s_copy(g, there, here):
        return pltpu.make_async_remote_copy(
            src_ref=ssend.at[g, there],
            dst_ref=srecv[g].at[here],
            send_sem=ss_sem.at[g, there],
            recv_sem=sr_sem.at[g, here],
            device_id={"ctx": there},
            device_id_type=MESH,
        )

    def a_copy(g, there, here):
        return pltpu.make_async_remote_copy(
            src_ref=att.at[here, g],
            dst_ref=att.at[here, g],
            send_sem=as_sem.at[there, g],
            recv_sem=ar_sem.at[here, g],
            device_id={"head": there},
            device_id_type=MESH,
        )

    fill_tables(n, tiles, sel, tblv)
    to_scalars = pltpu.make_async_copy(tblv, tbl, load_sem.at[4])
    to_scalars.start()
    loads[0].wait()
    to_scalars.wait()
    pl.semaphore_wait(barrier, n - 1 + nh - 1)

    def send_group(g):
        def send_queries(i, _):
            there = member(level - distance(i // TEAM), lax.rem(i, TEAM))

            @pl.when((there >= 0) & (there < me))
            def _():
                for hh in range(per):
                    h = g * per + hh
                    for s in range(CAP):
                        tile = tbl[0, h, there * CAP + s]
                        qsend[g, there, hh, s] = q[tile, :, h * width : (h + 1) * width]
                q_copy(g, there, me).start()

            return 0

        lax.fori_loop(0, n + TEAM, send_queries, 0)

    for g in range(min(AHEAD, groups)):
        send_group(g)
    loads[1].wait()
    loads[2].wait()
    causal = lax.broadcasted_iota(jnp.int32, (tokens, tokens), 0) >= lax.broadcasted_iota(
        jnp.int32, (tokens, tokens), 1
    )
    def own_group(g):
        for h in range(g * per, (g + 1) * per):
            cols = slice(h * width, (h + 1) * width)
            query = q[:, :, cols].reshape(tokens, width)
            part, top, total = softmax_block(query, k[:, cols], v[:, cols], scale, causal)
            lse = top * scale + jnp.log(total)
            own[h] = part.reshape(tiles, rows, width)
            own_lse[h] = jnp.broadcast_to(lse, (tokens, width)).reshape(tiles, rows, width)

    short = CAP * rows
    stat_lanes = ssend.shape[3]
    lane = lax.broadcasted_iota(jnp.int32, (TEAM, short, 128), 2)
    lane = lane - lax.broadcasted_iota(jnp.int32, (TEAM, short, 128), 1)

    def as_row(hit, column):
        column = jnp.broadcast_to(column, (TEAM * short, 128)).reshape(TEAM, short, 128)
        return jnp.sum(jnp.where(hit, column, 0.0), axis=1, keepdims=True)

    def answer_group(g):
        orecv[g][me] = jnp.zeros((per, CAP, rows, width), jnp.bfloat16)
        srecv[g][me] = jnp.full((1, stat_lanes), -1e30, jnp.float32)

        def answer(i, _):
            their = level + distance(i)

            @pl.when(their < levels)
            def _():
                for j in range(TEAM):
                    there = member(their, j)

                    @pl.when(there > me)
                    def _():
                        q_copy(g, me, there).wait_recv()

                team = pl.ds(pl.multiple_of(their * TEAM, TEAM), TEAM)
                both = 128 // short
                for first in range(0, per, both):
                    tops = jnp.zeros((TEAM, 1, 128), jnp.float32)
                    totals = jnp.zeros((TEAM, 1, 128), jnp.float32)
                    for hh in range(first, min(first + both, per)):
                        h = g * per + hh
                        cols = slice(h * width, (h + 1) * width)
                        query = qrecv[g][team, hh].reshape(TEAM * short, width)
                        part, top, total = softmax_block(query, k[:, cols], v[:, cols], scale, None)
                        part = part.astype(jnp.bfloat16).reshape(TEAM, CAP, rows, width)
                        osend[g, team, hh] = part
                        hit = lane == (hh - first) * short
                        tops += as_row(hit, top)
                        totals += as_row(hit, total)
                    ssend[g, team, :, first * short : first * short + 128] = tops * scale + jnp.log(
                        totals
                    )
                for j in range(TEAM):
                    there = member(their, j)

                    @pl.when(there > me)
                    def _():
                        o_copy(g, there, me).start()
                        s_copy(g, there, me).start()

            return 0

        lax.fori_loop(0, levels + 1, answer, 0)

    part_cols = min(256, out_ref.shape[1])

    def project(p, last):
        def body(c, _):
            at = pl.ds(pl.multiple_of(c * part_cols, part_cols), part_cols)
            term = 0.0 if p is hd else acc[:, at]
            for g in range(groups):
                term += jnp.dot(att[p, g], w[p, g, :, at], preferred_element_type=jnp.float32)
            if last:
                out_ref[:, at] = term.astype(out_ref.dtype)
            else:
                acc[:, at] = term
            return 0

        lax.fori_loop(0, out_ref.shape[1] // part_cols, body, 0)

    lane_tile = lax.broadcasted_iota(jnp.int32, (rows, 128), 1)
    lane_tile = lane_tile - lax.broadcasted_iota(jnp.int32, (rows, 128), 0)

    def collect_group(g):
        def collect(i, _):
            there = member(level - distance(i // TEAM), lax.rem(i, TEAM))

            @pl.when((there >= 0) & (there < me))
            def _():
                s_copy(g, me, there).wait_recv()
                o_copy(g, me, there).wait_recv()

            return 0

        lax.fori_loop(0, n + TEAM, collect, 0)

        def picked_lse(block, slot, hh):
            at = hh * short // 128 * 128
            hit = lane_tile == hh * short - at + slot * rows
            row = srecv[g][block][:, at : at + 128]
            return jnp.sum(jnp.where(hit, row, 0.0), axis=1, keepdims=True)

        for hh in range(per):
            h = g * per + hh

            def gather(r):
                blocks = [tbl[1, h, (r - 1) * tiles + t] for t in range(tiles)]
                slots = [tbl[2, h, (r - 1) * tiles + t] for t in range(tiles)]
                outs = [orecv[g][a, hh, s] for a, s in zip(blocks, slots)]
                lses = [picked_lse(a, s, hh) for a, s in zip(blocks, slots)]
                return jnp.concatenate(outs, 0).astype(jnp.float32), jnp.concatenate(lses, 0)

            (o1, l1), (o2, l2) = gather(1), gather(2)
            l0 = own_lse[h].reshape(tokens, width)
            top = jnp.maximum(l0, jnp.maximum(l1, l2))
            w0, w1, w2 = jnp.exp(l0 - top), jnp.exp(l1 - top), jnp.exp(l2 - top)
            mixed = w0 * own[h].reshape(tokens, width) + w1 * o1 + w2 * o2
            mixed = mixed / (w0 + w1 + w2)
            att[hd, g, :, hh * width : (hh + 1) * width] = mixed.astype(jnp.bfloat16)
        for j in range(1, nh):
            a_copy(g, lax.rem(hd + j, nh), hd).start()

    own_group(0)
    for g in range(groups):
        answer_group(g)
        if g + AHEAD < groups:
            send_group(g + AHEAD)
        if g + 1 < groups:
            own_group(g + 1)
        if g >= LAG:
            collect_group(g - LAG)
    for g in range(max(groups - LAG, 0), groups):
        collect_group(g)
    loads[3].wait()
    project(hd, nh == 1)
    for g in range(groups):

        def drain(d, _, g=g):
            @pl.when(me - d >= 0)
            def _():
                q_copy(g, me - d, me).wait_send()

            @pl.when(me + d < n)
            def _():
                o_copy(g, me + d, me).wait_send()
                s_copy(g, me + d, me).wait_send()

            return 0

        lax.fori_loop(1, n, drain, 0)

    for j in range(1, nh):
        peer = lax.rem(hd + j, nh)
        for g in range(groups):
            a_copy(g, hd, peer).wait_recv()
        project(peer, j == nh - 1)

    for g in range(groups):
        for j in range(1, nh):
            a_copy(g, lax.rem(hd + j, nh), hd).wait_send()


def solution(mesh):
    n, nh = mesh.shape["ctx"], mesh.shape["head"]

    def local(queries, keys, values, selected, out_weight):
        heads, tiles = selected.shape[:2]
        tokens, cols = queries.shape[0], out_weight.shape[1]
        width = queries.shape[1] // heads
        rows = tokens // tiles
        per = 2 if heads % 4 == 0 else 1
        groups = heads // per
        stat_lanes = -(-per * CAP * rows // 128) * 128
        table = (3, heads, -(-max(n * CAP, tiles * 3) // 128) * 128)
        bf16, f32 = jnp.bfloat16, jnp.float32
        dma = pltpu.SemaphoreType.DMA
        packet = (n, per, CAP, rows, width)
        grouped = (
            [pltpu.VMEM(packet, bf16)] * (2 * groups)
            + [pltpu.VMEM((n, 1, stat_lanes), f32)] * groups
        )
        weight = out_weight.reshape(nh, groups, per * width, cols)
        return pl.pallas_call(
            functools.partial(kernel, (n, nh, heads, tiles, rows, width, groups)),
            out_shape=jax.ShapeDtypeStruct((tokens, cols), bf16),
            in_specs=[pl.BlockSpec(memory_space=pltpu.VMEM)]
            + [pl.BlockSpec(memory_space=pl.ANY)] * 4,
            out_specs=pl.BlockSpec(memory_space=pltpu.VMEM),
            scratch_shapes=[
                pltpu.VMEM((tiles, rows, heads * width), bf16),
                pltpu.VMEM((tokens, heads * width), bf16),
                pltpu.VMEM((tokens, heads * width), bf16),
                pltpu.VMEM(weight.shape, bf16),
                pltpu.VMEM((groups,) + packet, bf16),
                pltpu.VMEM((groups,) + packet, bf16),
                pltpu.VMEM((groups, n, 1, stat_lanes), f32),
                pltpu.VMEM((heads, tiles, rows, width), f32),
                pltpu.VMEM((heads, tiles, rows, width), f32),
                pltpu.VMEM((nh, groups, tokens, per * width), bf16),
                pltpu.VMEM((tokens, cols), f32),
                pltpu.VMEM(table, jnp.int32),
                pltpu.SMEM(table, jnp.int32),
                dma((5,)),
                dma((groups, n)),
                dma((groups, n)),
                dma((groups, n)),
                dma((groups, n)),
                dma((groups, n)),
                dma((groups, n)),
                dma((nh, groups)),
                dma((nh, groups)),
            ]
            + grouped,
            compiler_params=pltpu.CompilerParams(
                collective_id=0, has_side_effects=True, vmem_limit_bytes=56 * 1024 * 1024
            ),
        )(
            jnp.transpose(selected, (2, 0, 1)),
            queries.reshape(tiles, rows, heads * width),
            keys,
            values,
            weight,
        )

    return jax.shard_map(
        local,
        mesh=mesh,
        in_specs=(
            P("ctx", "head"),
            P("ctx", "head"),
            P("ctx", "head"),
            P("head", "ctx", None),
            P(None, "head"),
        ),
        out_specs=P("ctx", "head"),
        check_vma=False,
    )
```
